512 devices in a mesh: tm: 16 (over z, core), space: 32 (over x, y).
Axes of the slice: x: 4, y: 8, z: 8, core: 2. Of those that a mesh axis runs over, the one named last changes fastest.
Arguments:
- right_side: float32 [1536, 8192], P('tm', 'space'), may hold values from -6 to 6
- obs_precision: float32 [1536, 8192], P('tm', 'space'), may hold values from 0.2 to 2
- mass_blocks: bfloat16 [64, 4, 128, 128], P('space')
- stiff_blocks: bfloat16 [64, 4, 128, 128], P('space')
- block_pattern: int32 [64, 4], P('space'), may hold values from 0 to 3, as said below
- send_lists: int32 [32, 2, 1], replicated, may hold values from 0 to 1, as said below
- time_bands: float32 [2, 3, 1536], replicated, as said below
Outputs:
- solution: float32 [1536, 8192], P('tm', 'space')
- residual: float32 [1536, 8192], P('tm', 'space')
The draws below stay inside these ranges and needn't reach their ends.
Inputs may be any that keep to these rules, and one draw needn't show every extreme that they name: `block_pattern`: column 0 of block row b holds b mod 2; columns 2 and 3 hold local numbers; column 1 holds a code of a neighbour's list. The pattern is mirrored: if row b names block c in column j, row c names block b in column j. `send_lists`: the two lists of a partition together hold each of its local block numbers once. `time_bands`: per row and matrix, band 0 exceeds twice the sum of the magnitudes of bands 1 and 2.
All inputs are finite; a program needn't handle non-finite values.
Results may differ from the reference program's by a relative error of at most 0.0003.
Values sent between devices are 32-bit elements; how exact they have to be, the bound alone decides.
No kernel may reach another device: no remote copies, remote signals or barrier semaphores. Data moves between devices by JAX's collectives and lax.ppermute only.
A program may use at most 64 MiB of HBM per device.

```python
import jax
import jax.numpy as jnp
from jax import lax

BLOCK = 128
NB = 4
ITERS = 4
BLK_DEV = 2
HB = 1
NPART = 32
SBLK = 64
NS = 8192
NT = 1536


def local_partner(perms):
    places = jnp.argsort(perms, axis=1, stable=True).astype(jnp.int32)
    flipped = jnp.bitwise_xor(places, 1)
    return jnp.take_along_axis(perms, flipped, axis=1).astype(jnp.int32)


def shared_pattern(key):
    list_key = jax.random.fold_in(key, 21)
    first_key = jax.random.fold_in(key, 23)
    second_key = jax.random.fold_in(key, 25)
    half_count = BLK_DEV // 2

    def permute_all(base):
        return jax.vmap(lambda subkey: jax.random.permutation(subkey, BLK_DEV))(jax.random.split(base, NPART)).astype(jnp.int32)
    orders = permute_all(list_key)
    send_lists = orders.reshape(NPART, 2, half_count)
    places = jnp.argsort(orders, axis=1, stable=True).astype(jnp.int32)
    part_ids = jnp.arange(NPART, dtype=jnp.int32)[:, None]
    lower_part = (part_ids - 1) % NPART
    upper_part = (part_ids + 1) % NPART
    low_index = jnp.clip(places, 0, half_count - 1)
    high_index = jnp.clip(places - half_count, 0, half_count - 1)
    lower_target = jnp.take_along_axis(orders[lower_part[:, 0]], half_count + low_index, axis=1)
    upper_target = jnp.take_along_axis(orders[upper_part[:, 0]], high_index, axis=1)
    goes_lower = places < half_count
    cross_code = jnp.where(goes_lower, BLK_DEV + low_index, BLK_DEV + half_count + high_index)
    cross_global = jnp.where(goes_lower, lower_part * BLK_DEV + lower_target, upper_part * BLK_DEV + upper_target)
    first_local = local_partner(permute_all(first_key))
    second_local = local_partner(permute_all(second_key))
    own_local = jnp.broadcast_to(jnp.arange(BLK_DEV, dtype=jnp.int32)[None, :], (NPART, BLK_DEV))
    codes = jnp.stack([own_local, cross_code, first_local, second_local], axis=-1)
    base = part_ids * BLK_DEV
    partners = jnp.stack([base + own_local, cross_global, base + first_local, base + second_local], axis=-1)
    return (send_lists.astype(jnp.int32), codes.reshape(SBLK, NB).astype(jnp.int32), partners.reshape(SBLK, NB).astype(jnp.int32))


def symmetric_blocks(key, partners):
    noise_key, diagonal_key = jax.random.split(key)
    block_shape = (SBLK, NB, BLOCK, BLOCK)
    noise_part = jax.random.normal(noise_key, block_shape, jnp.float32)
    noise_part = noise_part * (0.7 / (NB * BLOCK) ** 0.5)
    slot_ids = jnp.arange(NB, dtype=jnp.int32)[None, :]
    row_ids = jnp.arange(SBLK, dtype=jnp.int32)[:, None]
    mirrored = jnp.swapaxes(noise_part[partners, jnp.broadcast_to(slot_ids, partners.shape)], -1, -2)
    blocks = jnp.where((row_ids < partners)[:, :, None, None], noise_part, mirrored)
    own_noise = noise_part[:, 0]
    own_block = 0.5 * (own_noise + jnp.swapaxes(own_noise, -1, -2))
    diagonal = jax.random.uniform(diagonal_key, (SBLK, BLOCK), jnp.float32, 2.5, 4.0)
    identity = jnp.eye(BLOCK, dtype=jnp.float32)
    blocks = blocks.at[:, 0].set(own_block + diagonal[:, :, None] * identity[None])
    return blocks.astype(jnp.bfloat16)


def draw_block_pattern(key, part):
    send_lists, codes, partners = shared_pattern(key)
    return codes


def draw_send_lists(key, part):
    send_lists, codes, partners = shared_pattern(key)
    return send_lists


def draw_mass_blocks(key, part):
    send_lists, codes, partners = shared_pattern(key)
    key = jax.random.fold_in(key, 7)
    return symmetric_blocks(key, partners)


def draw_stiff_blocks(key, part):
    send_lists, codes, partners = shared_pattern(key)
    key = jax.random.fold_in(key, 9)
    return symmetric_blocks(key, partners)


def draw_time_bands(key, part):
    key = jax.random.fold_in(key, 11)
    main_key, first_key, second_key = jax.random.split(key, 3)
    main_band = jax.random.uniform(main_key, (2, NT), jnp.float32, 2.6, 4.0)
    first_band = jax.random.uniform(first_key, (2, NT), jnp.float32, -0.8, -0.2)
    second = jax.random.uniform(second_key, (2, NT), jnp.float32, 0.05, 0.3)
    return jnp.stack([main_band, first_band, second], axis=1)


def levels(rng, shape, shards, smallest, largest):
    gain, own = 1.0, jax.random.fold_in(rng, 6)
    for dim, blocks in shards:
        heights = jnp.exp(jax.random.uniform(jax.random.fold_in(own, dim), (blocks,), jnp.float32, smallest / len(shards), largest / len(shards)))
        gain = gain * jnp.repeat(heights, shape[dim] // blocks).reshape([-1 if axis == dim else 1 for axis in range(len(shape))])
    return gain


def gaussian(own_key, dims, spread, limit, cuts=(), kind=jnp.bfloat16):
    level = levels(own_key, dims, cuts, -0.22, 0.18) if cuts else 1.0
    array = jax.random.normal(own_key, dims, jnp.float32) * spread * level
    return jnp.minimum(jnp.maximum(array, -limit), limit).astype(kind)


def setup_inputs(seed: int = 0) -> dict:
    streams_of = jax.random.split(jax.random.key(seed), 8)
    right_side = gaussian(streams_of[0], (NT, NS), 1.0, 6.0, ((0, 16), (1, 32)), jnp.float32)
    obs_precision = jnp.clip(0.2 + 1.8 * jax.random.uniform(streams_of[1], (NT, NS), jnp.float32) ** levels(streams_of[1], (NT, NS), ((0, 16), (1, 32)), -0.2, 0.2), 0.2, 2.0)
    mass_blocks = draw_mass_blocks(jax.random.fold_in(streams_of[7], 71), 0)
    stiff_blocks = draw_stiff_blocks(jax.random.fold_in(streams_of[7], 71), 0)
    block_pattern = draw_block_pattern(jax.random.fold_in(streams_of[7], 71), 0)
    send_lists = draw_send_lists(jax.random.fold_in(streams_of[7], 71), 0)
    time_bands = draw_time_bands(jax.random.fold_in(streams_of[7], 71), 0)
    return dict(right_side=right_side, obs_precision=obs_precision, mass_blocks=mass_blocks, stiff_blocks=stiff_blocks, block_pattern=block_pattern, send_lists=send_lists, time_bands=time_bands)


def band_apply(band_rows, padded, length):
    centre = band_rows[:, 2:length + 2]
    result = centre[0][:, None] * padded[2:length + 2]
    result = result + centre[1][:, None] * padded[3:length + 3]
    result = result + band_rows[1, 1:length + 1][:, None] * padded[1:length + 1]
    result = result + centre[2][:, None] * padded[4:length + 4]
    result = result + band_rows[2, 0:length][:, None] * padded[0:length]
    return result


def resolve(block_pattern, send_lists):
    part_of_row = (jnp.arange(SBLK) // BLK_DEV).astype(jnp.int32)[:, None]
    lower_part = (part_of_row - 1) % NPART
    upper_part = (part_of_row + 1) % NPART
    lower_code = jnp.clip(block_pattern - BLK_DEV, 0, HB - 1)
    upper_code = jnp.clip(block_pattern - BLK_DEV - HB, 0, HB - 1)
    from_lower = lower_part * BLK_DEV + send_lists[lower_part, 1, lower_code]
    from_upper = upper_part * BLK_DEV + send_lists[upper_part, 0, upper_code]
    own_block = part_of_row * BLK_DEV + block_pattern
    inner = jnp.where(block_pattern < BLK_DEV + HB, from_lower, from_upper)
    return jnp.where(block_pattern < BLK_DEV, own_block, inner).astype(jnp.int32)


def spatial(vector, blocks, columns):
    node_tiles = vector.reshape(NT, SBLK, BLOCK)
    result = jnp.zeros((NT, SBLK, BLOCK), jnp.float32)
    for column in range(NB):
        picked = node_tiles[:, columns[:, column]]
        result = result + jnp.einsum("tbc,brc->tbr", picked, blocks[:, column].astype(jnp.float32), precision=lax.Precision.HIGHEST)
    return result.reshape(NT, NS)


def operate(vector, obs_precision, mass_blocks, stiff_blocks, columns, band_padded):
    mass_part = jnp.pad(spatial(vector, mass_blocks, columns), ((2, 2), (0, 0)))
    stiff_part = jnp.pad(spatial(vector, stiff_blocks, columns), ((2, 2), (0, 0)))
    result = band_apply(band_padded[0], mass_part, NT) + band_apply(band_padded[1], stiff_part, NT)
    return result + obs_precision * vector


def reference(right_side, obs_precision, mass_blocks, stiff_blocks, block_pattern, send_lists, time_bands):
    columns = resolve(block_pattern, send_lists)
    band_padded = jnp.pad(time_bands, ((0, 0), (0, 0), (2, 2)))
    mass_diag = jnp.diagonal(mass_blocks[:, 0].astype(jnp.float32), axis1=1, axis2=2).reshape(-1)
    stiff_diag = jnp.diagonal(stiff_blocks[:, 0].astype(jnp.float32), axis1=1, axis2=2).reshape(-1)
    precond = time_bands[0, 0][:, None] * mass_diag[None, :] + time_bands[1, 0][:, None] * stiff_diag[None, :] + obs_precision
    solution = jnp.zeros_like(right_side)
    residual = right_side
    scaled = residual / precond
    direction = scaled
    norm_now = jnp.sum(residual * scaled)
    for iteration in range(ITERS):
        applied = operate(direction, obs_precision, mass_blocks, stiff_blocks, columns, band_padded)
        step_size = norm_now / jnp.sum(direction * applied)
        solution = solution + step_size * direction
        residual = residual - step_size * applied
        if iteration + 1 < ITERS:
            scaled = residual / precond
            norm_next = jnp.sum(residual * scaled)
            direction = scaled + (norm_next / norm_now) * direction
            norm_now = norm_next
    return solution, residual
```

```python
import jax
import jax.numpy as jnp
from jax import lax
from jax.experimental import pallas as pl
from jax.experimental.pallas import tpu as pltpu
from jax.sharding import PartitionSpec as P

ITERS = 4
HALO = 2 * ITERS
BLOCK = 128
CENTRE = 1.0
WIDTH = 0.6
VMEM = pl.BlockSpec(memory_space=pltpu.VMEM)
SMEM = pl.BlockSpec(memory_space=pltpu.SMEM)
F32 = jnp.float32


def column(bands, index):
    return bands[:, index : index + 1]


def product(pieces, weights):
    return jnp.dot(
        jnp.concatenate(pieces, axis=1),
        jnp.concatenate(weights, axis=0),
        precision=lax.Precision.HIGHEST,
        preferred_element_type=F32,
    )


def moved(rows, offset):
    return pltpu.roll(rows, (-offset) % rows.shape[0], 0)


def band_apply(bands, base, rows):
    result = column(bands, base) * rows
    result = result + column(bands, base + 1) * moved(rows, 1)
    result = result + column(bands, base + 2) * moved(rows, -1)
    result = result + column(bands, base + 3) * moved(rows, 2)
    return result + column(bands, base + 4) * moved(rows, -2)


def image(bands, spatial, precision, vector):
    return (
        band_apply(bands, 0, spatial[:, :BLOCK])
        + band_apply(bands, 5, spatial[:, BLOCK:])
        + precision * vector
    )


def prepare_kernel(
    meta, right, obs, before, after, mass, stiff, bands_ref,
    scaled_ref, precond_ref, obs_ref, weights_ref, up_ref, down_ref,
):
    low = meta[0]
    high = 1 - low
    swapped = low == 1
    rows = right.shape[0]
    bands = bands_ref[...]
    valid = column(bands, 10)
    rhs = jnp.concatenate([before[:HALO], right[...], after[:HALO]], axis=0)
    precision = jnp.concatenate([before[HALO:], obs[...], after[HALO:]], axis=0)
    eye = lax.broadcasted_iota(jnp.int32, (BLOCK, BLOCK), 0) == lax.broadcasted_iota(
        jnp.int32, (BLOCK, BLOCK), 1
    )
    own = (low, high)

    def chain(array):
        first, second = array[:, :BLOCK], array[:, BLOCK:]
        return jnp.where(swapped, second, first), jnp.where(swapped, first, second)

    rhs, precision = chain(rhs), chain(precision)
    extent = rhs[0].shape[0]
    for place in range(2):
        block = own[place]
        diagonals = [
            jnp.sum(jnp.where(eye, ref[block, 0].astype(F32), 0.0), axis=0, keepdims=True)
            for ref in (mass, stiff)
        ]
        precond = column(bands, 0) * diagonals[0] + column(bands, 5) * diagonals[1]
        precond = precond + precision[place] + (1.0 - valid)
        scaled = valid * rhs[place] / precond
        lanes = slice(place * BLOCK, (place + 1) * BLOCK)
        scaled_ref[:, lanes] = scaled
        precond_ref[:, lanes] = precond
        obs_ref[:, lanes] = precision[place]
        near, far = ((down_ref, up_ref), (up_ref, down_ref))[place]
        near[:extent] = scaled
        far[extent : 2 * extent] = scaled
        near[2 * extent : 3 * extent] = precision[place]
        near[3 * extent : 3 * extent + 8] = jnp.concatenate(
            diagonals + [jnp.zeros((6, BLOCK), F32)], axis=0
        )
    start = 3 * extent + 8
    for index, ref in enumerate((mass, stiff)):
        lanes = slice(index * BLOCK, (index + 1) * BLOCK)

        def total(row, col):
            result = ref[own[row], 0].astype(F32) if row == col else jnp.zeros((BLOCK, BLOCK), F32)
            for j in (2, 3):
                named = meta[1 + own[row] * 4 + j] == own[col]
                result = result + jnp.where(named, ref[own[row], j].astype(F32), 0.0)
            return result

        first, second = total(0, 0), total(1, 1)
        first_second, second_first = total(0, 1), total(1, 0)
        cross_low = ref[low, 1].astype(F32)
        cross_high = ref[high, 1].astype(F32)
        parts = (
            first, second_first, cross_low.T,
            first_second, second, cross_high.T,
            cross_low, cross_high,
        )
        for place, part in enumerate(parts):
            weights_ref[place, :, lanes] = part
        place = start + index * BLOCK
        up_ref[place : place + BLOCK] = first_second
        up_ref[place + 2 * BLOCK : place + 3 * BLOCK] = second
        down_ref[place : place + BLOCK] = second_first
        down_ref[place + 2 * BLOCK : place + 3 * BLOCK] = first


def ghost(bands, ref):
    extent = bands.shape[0]
    near, far = ref[:extent], ref[extent : 2 * extent]
    precision = ref[2 * extent : 3 * extent]
    start = 3 * extent
    precond = column(bands, 0) * ref[start : start + 1]
    precond = precond + column(bands, 5) * ref[start + 1 : start + 2]
    precond = precond + precision + (1.0 - column(bands, 10))
    start = start + 8
    blocks = [ref[start + k * BLOCK : start + (k + 1) * BLOCK] for k in range(4)]
    weights = [
        jnp.concatenate(blocks[:2], axis=1),
        jnp.concatenate(blocks[2:], axis=1),
    ]
    return near, far, precision, precond, weights


def halves(ref):
    return ref[:, :BLOCK], ref[:, BLOCK:]


def stepped(bands, spatial, precision, precond, vector, older):
    applied = image(bands, spatial, precision, vector)
    shifted = column(bands, 10) * applied / precond - CENTRE * vector
    if older is None:
        return shifted * (1.0 / WIDTH)
    return shifted * (2.0 / WIDTH) - older


def first_kernel(
    scaled, precond_ref, obs, weights, below, above, bands_ref,
    one_ref, two_ref, near_ref,
):
    bands = bands_ref[...]
    vector, precond, precision = halves(scaled), halves(precond_ref), halves(obs)
    sides = (ghost(bands, below), ghost(bands, above))
    outer = []
    for place, (near, far, near_obs, near_precond, side) in enumerate(sides):
        spatial = product([far, near, vector[place]], side + [weights[6 + place]])
        outer.append(stepped(bands, spatial, near_obs, near_precond, near, None))
        near_ref[place] = outer[place]
    inner = []
    for place in range(2):
        spatial = product(
            list(vector) + [sides[place][0]], [weights[3 * place + k] for k in range(3)]
        )
        inner.append(stepped(bands, spatial, precision[place], precond[place], vector[place], None))
        one_ref[place] = inner[place]
    for place in range(2):
        spatial = product(inner + [outer[place]], [weights[3 * place + k] for k in range(3)])
        two_ref[place] = stepped(
            bands, spatial, precision[place], precond[place], inner[place], vector[place]
        )


def second_kernel(
    scaled, one_ref, two_ref, near_ref, precond_ref, obs, weights, below, above, bands_ref,
    below_two, above_two, three_ref, four_ref, sums_ref,
):
    bands = bands_ref[...]
    precond, precision = halves(precond_ref), halves(obs)
    extent = bands.shape[0]
    two = (two_ref[0], two_ref[1])
    nears = (below_two[1], above_two[0])
    fars = (below_two[0], above_two[1])
    outer = []
    for place, ref in enumerate((below, above)):
        _, _, near_obs, near_precond, side = ghost(bands, ref)
        spatial = product([fars[place], nears[place], two[place]], side + [weights[6 + place]])
        outer.append(
            stepped(bands, spatial, near_obs, near_precond, nears[place], near_ref[place])
        )
    three = []
    for place in range(2):
        spatial = product(list(two) + [nears[place]], [weights[3 * place + k] for k in range(3)])
        three.append(
            stepped(bands, spatial, precision[place], precond[place], two[place], one_ref[place])
        )
        three_ref[place] = three[place]
    sums = [0.0] * 14
    inside = slice(HALO, extent - HALO)
    start = halves(scaled)
    for place in range(2):
        spatial = product(three + [outer[place]], [weights[3 * place + k] for k in range(3)])
        four = stepped(bands, spatial, precision[place], precond[place], three[place], two[place])
        four_ref[place] = four
        basis = [
            rows[inside]
            for rows in (start[place], one_ref[place], two[place], three[place], four)
        ]
        index = 0
        for i in range(4):
            weighted = precond[place][inside] * basis[i]
            for j in range(i, 5):
                term = (weighted * basis[j]).reshape(-1, 8, BLOCK)
                sums[index] = sums[index] + jnp.sum(term, axis=0)
                index += 1
    rows = [jnp.sum(part, axis=0, keepdims=True) for part in sums]
    table = jnp.concatenate(rows + [jnp.zeros((2, BLOCK), F32)], axis=0)
    totals = jnp.sum(table, axis=1, keepdims=True)
    slots = lax.broadcasted_iota(jnp.int32, (16, BLOCK), 0) == lax.broadcasted_iota(
        jnp.int32, (16, BLOCK), 1
    )
    sums_ref[...] = jnp.sum(jnp.where(slots, totals, 0.0), axis=0, keepdims=True)


def operator(vector):
    result = [0.0] * 5
    for j in range(4):
        result[j] = result[j] + CENTRE * vector[j]
        if j == 0:
            result[1] = result[1] + WIDTH * vector[0]
        else:
            result[j + 1] = result[j + 1] + (0.5 * WIDTH) * vector[j]
            result[j - 1] = result[j - 1] + (0.5 * WIDTH) * vector[j]
    return result


def inner_product(table, left, right):
    total = 0.0
    for i, a in enumerate(left):
        for j, b in enumerate(right):
            if a is not None and b is not None:
                total = total + table[(min(i, j), max(i, j))] * (a * b)
    return total


def final_kernel(meta, parts, scaled, one_ref, two_ref, three_ref, four_ref, precond_ref,
                 solution_ref, residual_ref):
    rows = jnp.sum(parts[...], axis=0, keepdims=True)
    lane = lax.broadcasted_iota(jnp.int32, (1, BLOCK), 1)
    table = {}
    index = 0
    for i in range(4):
        for j in range(i, 5):
            table[(i, j)] = jnp.sum(jnp.where(lane == index, rows, 0.0), axis=1, keepdims=True)
            index += 1
    one = jnp.ones((1, 1), F32)
    zero = jnp.zeros((1, 1), F32)
    state = [one, zero, zero, zero, zero]
    direction = list(state)
    answer = [zero] * 5
    norm_now = table[(0, 0)]

    def cut(vector, degree):
        return [v if k <= degree else None for k, v in enumerate(vector)]

    for iteration in range(ITERS):
        applied = operator(direction)
        step = norm_now / inner_product(
            table, cut(direction, iteration), cut(applied, iteration + 1)
        )
        answer = [a + step * d for a, d in zip(answer, direction)]
        state = [s - step * w for s, w in zip(state, applied)]
        if iteration + 1 < ITERS:
            kept = cut(state, iteration + 1)
            norm_next = inner_product(table, kept, kept)
            direction = [s + norm_next / norm_now * d for s, d in zip(state, direction)]
            norm_now = norm_next
    swapped = meta[0] == 1
    precond = halves(precond_ref)
    start = halves(scaled)
    extent = start[0].shape[0]
    inside = slice(HALO, extent - HALO)
    solutions, residuals = [], []
    for place in range(2):
        basis = [
            rows[inside]
            for rows in (
                start[place], one_ref[place], two_ref[place], three_ref[place], four_ref[place]
            )
        ]
        total = answer[0] * basis[0]
        left = state[0] * basis[0]
        for k in range(1, 5):
            if k < 4:
                total = total + answer[k] * basis[k]
            left = left + state[k] * basis[k]
        solutions.append(total)
        residuals.append(left * precond[place][inside])
    for ref, pair in ((solution_ref, solutions), (residual_ref, residuals)):
        ref[:, :BLOCK] = jnp.where(swapped, pair[1], pair[0])
        ref[:, BLOCK:] = jnp.where(swapped, pair[0], pair[1])


def call(kernel, shapes, *operands, scalars=0):
    return pl.pallas_call(
        kernel,
        out_shape=[jax.ShapeDtypeStruct(shape, F32) for shape in shapes],
        in_specs=[SMEM] * scalars + [VMEM] * (len(operands) - scalars),
        out_specs=[VMEM] * len(shapes),
        compiler_params=pltpu.CompilerParams(vmem_limit_bytes=32 * 1024 * 1024),
    )(*operands)


def ring(array, axis, wrap):
    devices = lax.axis_size(axis)
    up = [(i, (i + 1) % devices) for i in range(devices if wrap else devices - 1)]
    return up, [(j, i) for i, j in up]


def shards(
    right_side, obs_precision, mass_blocks, stiff_blocks, block_pattern, send_lists, time_bands
):
    time_rows, nodes = right_side.shape
    extent = time_rows + 2 * HALO
    part = lax.axis_index("space")
    low = lax.dynamic_index_in_dim(send_lists, part, 0, keepdims=False)[0]
    meta = jnp.concatenate([low, block_pattern.reshape(-1)])

    up, down = ring(right_side, "tm", False)
    last = jnp.concatenate([right_side[-HALO:], obs_precision[-HALO:]], axis=0)
    first = jnp.concatenate([right_side[:HALO], obs_precision[:HALO]], axis=0)
    before = lax.ppermute(last, "tm", up)
    after = lax.ppermute(first, "tm", down)

    start = lax.axis_index("tm") * time_rows
    margin = HALO + 2
    known = jnp.ones((1, time_bands.shape[2]), F32)
    padded = jnp.concatenate([time_bands.reshape(6, -1), known], axis=0)
    padded = jnp.pad(padded, ((0, 0), (margin, margin)))
    local = lax.dynamic_slice_in_dim(padded, start, extent + 4, 1)
    lines = []
    for matrix in range(2):
        for band, offset in ((0, 0), (1, 0), (1, -1), (2, 0), (2, -2)):
            row = 3 * matrix + band
            lines.append(local[row, 2 + offset : 2 + offset + extent])
    lines.append(local[6, 2 : 2 + extent])
    bands = jnp.pad(jnp.stack(lines, axis=1), ((0, 0), (0, 16 - len(lines))))

    full = (extent, nodes)
    pair = (2, extent, BLOCK)
    buffer = (3 * extent + 8 + 4 * BLOCK, BLOCK)
    scaled, precond, precision, weights, to_up, to_down = call(
        prepare_kernel,
        [full, full, full, (8, BLOCK, 2 * BLOCK), buffer, buffer],
        meta, right_side, obs_precision, before, after, mass_blocks, stiff_blocks, bands,
        scalars=1,
    )
    up, down = ring(right_side, "space", True)
    below = lax.ppermute(to_up, "space", up)
    above = lax.ppermute(to_down, "space", down)
    one, two, near = call(
        first_kernel, [pair, pair, pair], scaled, precond, precision, weights, below, above, bands
    )
    below_two = lax.ppermute(two, "space", up)
    above_two = lax.ppermute(two, "space", down)
    three, four, sums = call(
        second_kernel,
        [pair, pair, (1, BLOCK)],
        scaled, one, two, near, precond, precision, weights, below, above, bands,
        below_two, above_two,
    )
    for axis in ("space", "tm"):
        devices = lax.axis_size(axis)
        sent = jnp.broadcast_to(sums[None], (devices, 1, BLOCK))
        parts = lax.all_to_all(sent, axis, 0, 0)
        sums = jnp.sum(parts, axis=0)
    return tuple(
        call(
            final_kernel,
            [right_side.shape, right_side.shape],
            meta, sums, scaled, one, two, three, four, precond,
            scalars=1,
        )
    )


def solution(mesh):
    placed = (
        P("tm", "space"),
        P("tm", "space"),
        P("space", None, None, None),
        P("space", None, None, None),
        P("space", None),
        P(),
        P(),
    )
    return jax.shard_map(
        shards,
        mesh=mesh,
        in_specs=placed,
        out_specs=(P("tm", "space"), P("tm", "space")),
        check_vma=False,
    )
```

```python
import jax
import jax.numpy as jnp
from jax import lax
from jax.experimental import pallas as pl
from jax.experimental.pallas import tpu as pltpu
from jax.sharding import PartitionSpec as P

ITERS = 4
HALO = 2 * ITERS
BLOCK = 128
CENTRE = 1.0
WIDTH = 0.6
VMEM = pl.BlockSpec(memory_space=pltpu.VMEM)
SMEM = pl.BlockSpec(memory_space=pltpu.SMEM)
F32 = jnp.float32
BF16 = jnp.bfloat16
TERMS = ((0, 0), (1, 0), (1, -1), (2, 0), (2, -2))


def parts_of(array, count):
    parts = []
    for _ in range(count):
        part = array.astype(BF16)
        parts.append(part)
        array = array - part.astype(F32)
    return parts


def dot(left, right):
    return jnp.dot(left, right, preferred_element_type=F32)


def local_product(vectors, weights):
    first, second, third = parts_of(jnp.concatenate(vectors, axis=1), 3)
    return dot(
        jnp.concatenate([first, second, third, first, second], axis=1), weights[...]
    )


def cross_product(vector, block):
    return dot(
        jnp.concatenate(parts_of(vector, 3), axis=1), jnp.concatenate([block] * 3, axis=0)
    )


def moved(rows, offset):
    return pltpu.roll(rows, (-offset) % rows.shape[0], 0)


def band_apply(bands, spatial):
    result = None
    for matrix in range(2):
        rows = spatial[:, matrix * BLOCK : (matrix + 1) * BLOCK]
        for index, offset in enumerate((0, 1, -1, 2, -2)):
            term = bands[5 * matrix + index] * (moved(rows, offset) if offset else rows)
            result = term if result is None else result + term
    return result


def weights_kernel(
    lists, pattern, bands_row, mass, stiff,
    bands_ref, flag_ref, diagonal_ref, local_ref, into_ref, out_ref,
    *, time_rows, time_total,
):
    part = lax.axis_index("space")
    low = lists[0, 0, part]
    high = 1 - low
    own = (low, high)
    flag_ref[...] = jnp.full((8, BLOCK), low.astype(F32))
    extent = time_rows + 2 * HALO
    lines = []
    for matrix in range(2):
        for band, offset in TERMS:
            line = bands_row[band, matrix : matrix + 1, :]
            lines.append(pltpu.roll(line, (-(2 + offset)) % BLOCK, 1))
    lines.append(jnp.zeros((BLOCK - len(lines), BLOCK), F32))
    columns = jnp.concatenate(lines, axis=0).T
    for index in range(10):
        bands_ref[index] = jnp.broadcast_to(
            columns[:extent, index : index + 1], (extent, BLOCK)
        )
    time = lax.broadcasted_iota(jnp.int32, (extent, BLOCK), 0) - HALO
    time = time + lax.axis_index("tm") * time_rows
    bands_ref[10] = jnp.where((time >= 0) & (time < time_total), 1.0, 0.0)
    eye = lax.broadcasted_iota(jnp.int32, (BLOCK, BLOCK), 0) == lax.broadcasted_iota(
        jnp.int32, (BLOCK, BLOCK), 1
    )
    for place in range(2):
        for matrix, ref in enumerate((mass, stiff)):
            row = 2 * place + matrix
            diagonal_ref[row : row + 1] = jnp.sum(
                jnp.where(eye, ref[own[place], 0].astype(F32), 0.0), axis=0, keepdims=True
            )
    diagonal_ref[4:] = jnp.zeros((4, BLOCK), F32)
    for matrix, ref in enumerate((mass, stiff)):
        for col in range(2):
            lanes = slice((2 * col + matrix) * BLOCK, (2 * col + matrix + 1) * BLOCK)
            for row in range(2):
                if row == col:
                    total = ref[own[row], 0].astype(F32)
                else:
                    total = jnp.zeros((BLOCK, BLOCK), F32)
                for j in (2, 3):
                    named = pattern[own[row], j] == own[col]
                    total = total + jnp.where(named, ref[own[row], j].astype(F32), 0.0)
                lead, rest = parts_of(total, 2)
                for k, value in enumerate((lead, lead, lead, rest, rest)):
                    start = (2 * k + row) * BLOCK
                    local_ref[start : start + BLOCK, lanes] = value
        lanes = slice(matrix * BLOCK, (matrix + 1) * BLOCK)
        for place in range(2):
            block = ref[own[place], 1]
            out_ref[place, :, lanes] = block
            into_ref[place, :, lanes] = block.astype(F32).T.astype(BF16)


def stepped(scale, applied, inverse, vector, older):
    result = scale * (inverse * applied - CENTRE * vector)
    return result if older is None else result - older


def prepare_kernel(
    right, obs, before, after, bands, flag, diagonal, local,
    precond_ref, obs_ref, down_ref, up_ref,
):
    swapped = flag[0:1] > 0.5
    rhs = jnp.concatenate([before[:HALO], right[...], after[:HALO]], axis=0)
    precision = jnp.concatenate([before[HALO:], obs[...], after[HALO:]], axis=0)

    def chain(array):
        first, second = array[:, :BLOCK], array[:, BLOCK:]
        return jnp.where(swapped, second, first), jnp.where(swapped, first, second)

    rhs, precision = chain(rhs), chain(precision)
    valid = bands[10]
    scaled, inverses = [], []
    for place in range(2):
        precond = bands[0] * diagonal[2 * place : 2 * place + 1]
        precond = precond + bands[5] * diagonal[2 * place + 1 : 2 * place + 2]
        precond = precond + precision[place] + (1.0 - valid)
        precond_ref[place] = precond
        obs_ref[place] = precision[place]
        inverses.append(valid / precond)
        scaled.append(rhs[place] * inverses[place])
    spatial = local_product(scaled, local)
    for place, ref in enumerate((down_ref, up_ref)):
        applied = band_apply(bands, spatial[:, 2 * place * BLOCK : 2 * (place + 1) * BLOCK])
        applied = applied + precision[place] * scaled[place]
        ref[0] = scaled[place]
        ref[1] = stepped(1.0 / WIDTH, applied, inverses[place], scaled[place], None)
        ref[2] = inverses[place]


def completed(scale, bands, block, vector, partial, inverse):
    return partial + scale * (inverse * band_apply(bands, cross_product(vector, block)))


def full_step(bands, local, into, vectors, nears, precision, inverses, olders):
    spatial = local_product(vectors, local)
    results = []
    for place in range(2):
        mine = spatial[:, 2 * place * BLOCK : 2 * (place + 1) * BLOCK]
        mine = mine + cross_product(nears[place], into[place])
        applied = band_apply(bands, mine) + precision[place] * vectors[place]
        results.append(
            stepped(2.0 / WIDTH, applied, inverses[place], vectors[place], olders[place])
        )
    return results


def first_kernel(
    down, up, below, above, obs, bands, local, into, out,
    one_ref, down_two_ref, up_two_ref,
):
    own, sides = (down, up), (below, above)
    scale = 1.0 / WIDTH
    inverses = [ref[2] for ref in own]
    vectors = [
        completed(scale, bands, into[k], sides[k][0], own[k][1], inverses[k]) for k in range(2)
    ]
    nears = [
        completed(scale, bands, out[k], own[k][0], sides[k][1], sides[k][2]) for k in range(2)
    ]
    olders = [ref[0] for ref in own]
    two = full_step(bands, local, into, vectors, nears, obs, inverses, olders)
    spatial = local_product(two, local)
    for place, ref in enumerate((down_two_ref, up_two_ref)):
        one_ref[place] = vectors[place]
        applied = band_apply(bands, spatial[:, 2 * place * BLOCK : 2 * (place + 1) * BLOCK])
        applied = applied + obs[place] * two[place]
        ref[0] = two[place]
        ref[1] = stepped(2.0 / WIDTH, applied, inverses[place], two[place], vectors[place])


def second_kernel(
    down, up, below, above, one, down_two, up_two, below_two, above_two, precond, obs,
    bands, local, into, out,
    three_ref, four_ref, sums_ref,
):
    own, sides = (down, up), (below, above)
    own_two, sides_two = (down_two, up_two), (below_two, above_two)
    scale = 2.0 / WIDTH
    inverses = [ref[2] for ref in own]
    vectors = [
        completed(scale, bands, into[k], sides_two[k][0], own_two[k][1], inverses[k])
        for k in range(2)
    ]
    nears = [
        completed(scale, bands, out[k], own_two[k][0], sides_two[k][1], sides[k][2])
        for k in range(2)
    ]
    olders = [ref[0] for ref in own_two]
    four = full_step(bands, local, into, vectors, nears, obs, inverses, olders)
    extent = bands.shape[1]
    inside = slice(HALO, extent - HALO)
    sums = [0.0] * 14
    for place in range(2):
        three_ref[place] = vectors[place]
        four_ref[place] = four[place]
        basis = (own[place][0], one[place], olders[place], vectors[place], four[place])
        basis = [rows[inside] for rows in basis]
        index = 0
        for i in range(4):
            weighted = precond[place][inside] * basis[i]
            for j in range(i, 5):
                term = (weighted * basis[j]).reshape(-1, 8, BLOCK)
                sums[index] = sums[index] + jnp.sum(term, axis=0)
                index += 1
    rows = [jnp.sum(part, axis=0, keepdims=True) for part in sums]
    table = jnp.concatenate(rows + [jnp.zeros((2, BLOCK), F32)], axis=0)
    totals = jnp.sum(table, axis=1, keepdims=True)
    slots = lax.broadcasted_iota(jnp.int32, (16, BLOCK), 0) == lax.broadcasted_iota(
        jnp.int32, (16, BLOCK), 1
    )
    sums_ref[...] = jnp.sum(jnp.where(slots, totals, 0.0), axis=0, keepdims=True)


def added(terms):
    while len(terms) > 1:
        terms = [
            terms[k] + terms[k + 1] if k + 1 < len(terms) else terms[k]
            for k in range(0, len(terms), 2)
        ]
    return terms[0]


def operator(vector, degree):
    result = [[] for _ in range(5)]
    for j in range(degree + 1):
        result[j].append(CENTRE * vector[j])
        if j == 0:
            result[1].append(WIDTH * vector[0])
        else:
            result[j + 1].append((0.5 * WIDTH) * vector[j])
            result[j - 1].append((0.5 * WIDTH) * vector[j])
    return [added(terms) if terms else None for terms in result]


def inner_product(table, left, right):
    terms = []
    for i, a in enumerate(left):
        if a is not None:
            row = [
                table[(min(i, j), max(i, j))] * b for j, b in enumerate(right) if b is not None
            ]
            terms.append(a * added(row))
    return added(terms)


def combined(first, factor, second):
    result = []
    for a, b in zip(first, second):
        if b is None:
            result.append(a)
        else:
            result.append(factor * b if a is None else a + factor * b)
    return result


def final_kernel(
    flag, parts, down, up, one, down_two, up_two, three, four, precond,
    solution_ref, residual_ref,
):
    rows = jnp.sum(parts[...], axis=0, keepdims=True)
    lane = lax.broadcasted_iota(jnp.int32, (1, BLOCK), 1)
    table = {}
    index = 0
    for i in range(4):
        for j in range(i, 5):
            table[(i, j)] = jnp.sum(jnp.where(lane == index, rows, 0.0), axis=1, keepdims=True)
            index += 1
    state = [jnp.ones((1, 1), F32)] + [None] * 4
    direction = list(state)
    answer = [None] * 5
    norm_now = table[(0, 0)]
    for iteration in range(ITERS):
        applied = operator(direction, iteration)
        step = norm_now / inner_product(table, direction, applied)
        answer = combined(answer, step, direction)
        state = combined(state, -step, applied)
        if iteration + 1 < ITERS:
            norm_next = inner_product(table, state, state)
            direction = combined(state, norm_next / norm_now, direction)
            norm_now = norm_next
    swapped = flag[0:1] > 0.5
    inside = slice(HALO, HALO + solution_ref.shape[0])
    solutions, residuals = [], []
    for place, (ref, ref_two) in enumerate(((down, down_two), (up, up_two))):
        basis = (ref[0], one[place], ref_two[0], three[place], four[place])
        basis = [rows[inside] for rows in basis]
        solutions.append(added([answer[k] * basis[k] for k in range(4)]))
        left = added([state[k] * basis[k] for k in range(5)])
        residuals.append(left * precond[place][inside])
    for ref, pair in ((solution_ref, solutions), (residual_ref, residuals)):
        ref[:, :BLOCK] = jnp.where(swapped, pair[1], pair[0])
        ref[:, BLOCK:] = jnp.where(swapped, pair[0], pair[1])


def call(kernel, shapes, *operands, scalars=0, flops=0):
    return pl.pallas_call(
        kernel,
        out_shape=[
            shape if isinstance(shape, jax.ShapeDtypeStruct) else jax.ShapeDtypeStruct(shape, F32)
            for shape in shapes
        ],
        in_specs=[SMEM] * scalars + [VMEM] * (len(operands) - scalars),
        out_specs=[VMEM] * len(shapes),
        compiler_params=pltpu.CompilerParams(vmem_limit_bytes=32 * 1024 * 1024),
        cost_estimate=pl.CostEstimate(flops=flops, bytes_accessed=1 << 20, transcendentals=0),
    )(*operands)


def ring(axis, wrap):
    devices = lax.axis_size(axis)
    up = [(i, (i + 1) % devices) for i in range(devices if wrap else devices - 1)]
    return up, [(j, i) for i, j in up]


def shards(
    right_side, obs_precision, mass_blocks, stiff_blocks, block_pattern, send_lists, time_bands
):
    time_rows = right_side.shape[0]
    time_total = time_bands.shape[2]
    extent = time_rows + 2 * HALO

    up, down = ring("tm", False)
    last = jnp.concatenate([right_side[-HALO:], obs_precision[-HALO:]], axis=0)
    first = jnp.concatenate([right_side[:HALO], obs_precision[:HALO]], axis=0)
    before = lax.ppermute(last, "tm", up)
    after = lax.ppermute(first, "tm", down)

    margin = HALO + 2
    padded = jnp.pad(time_bands.transpose(1, 0, 2), ((0, 0), (0, 0), (margin, BLOCK)))
    bands_row = lax.dynamic_slice_in_dim(
        padded, lax.axis_index("tm") * time_rows, BLOCK, 2
    )
    wide = 2 * BLOCK
    bands, flag, diagonal, local, into, out = call(
        lambda *refs: weights_kernel(*refs, time_rows=time_rows, time_total=time_total),
        [
            (11, extent, BLOCK),
            (8, BLOCK),
            (8, BLOCK),
            jax.ShapeDtypeStruct((5 * wide, 2 * wide), BF16),
            jax.ShapeDtypeStruct((2, BLOCK, wide), BF16),
            jax.ShapeDtypeStruct((2, BLOCK, wide), BF16),
        ],
        send_lists.transpose(1, 2, 0), block_pattern, bands_row, mass_blocks, stiff_blocks,
        scalars=2, flops=1 << 21,
    )

    pair = (2, extent, BLOCK)
    triple = (3, extent, BLOCK)
    precond, precision, to_down, to_up = call(
        prepare_kernel, [pair, pair, triple, triple],
        right_side, obs_precision, before, after, bands, flag, diagonal, local,
    )
    up, down = ring("space", True)
    below = lax.ppermute(to_up, "space", up)
    above = lax.ppermute(to_down, "space", down)
    one, down_two, up_two = call(
        first_kernel, [pair, pair, pair],
        to_down, to_up, below, above, precision, bands, local, into, out,
    )
    below_two = lax.ppermute(up_two, "space", up)
    above_two = lax.ppermute(down_two, "space", down)
    three, four, sums = call(
        second_kernel, [pair, pair, (1, BLOCK)],
        to_down, to_up, below, above, one, down_two, up_two, below_two, above_two,
        precond, precision, bands, local, into, out,
    )
    for axis in ("space", "tm"):
        devices = lax.axis_size(axis)
        sent = jnp.broadcast_to(sums[None], (devices, 1, BLOCK))
        gathered = lax.all_to_all(sent, axis, 0, 0)
        sums = jnp.sum(gathered, axis=0)
    return tuple(
        call(
            final_kernel, [right_side.shape, right_side.shape],
            flag, sums, to_down, to_up, one, down_two, up_two, three, four, precond,
        )
    )


def solution(mesh):
    placed = (
        P("tm", "space"),
        P("tm", "space"),
        P("space", None, None, None),
        P("space", None, None, None),
        P("space", None),
        P(),
        P(),
    )
    return jax.shard_map(
        shards,
        mesh=mesh,
        in_specs=placed,
        out_specs=(P("tm", "space"), P("tm", "space")),
        check_vma=False,
    )
```

```python
import jax
import jax.numpy as jnp
from jax import lax
from jax.experimental import pallas as pl
from jax.experimental.pallas import tpu as pltpu
from jax.sharding import PartitionSpec as P

ITERS = 4
HALO = 2 * ITERS
BLOCK = 128
CENTRE = 1.0
WIDTH = 0.6
VMEM = pl.BlockSpec(memory_space=pltpu.VMEM)
F32 = jnp.float32
BF16 = jnp.bfloat16
TERMS = ((0, 0), (1, 0), (1, -1), (2, 0), (2, -2))


def parts_of(array, count):
    parts = []
    for _ in range(count):
        part = array.astype(BF16)
        parts.append(part)
        array = array - part.astype(F32)
    return parts


def dot(left, right):
    return jnp.dot(left, right, preferred_element_type=F32)


def local_product(vectors, weights):
    first, second, third = parts_of(jnp.concatenate(vectors, axis=1), 3)
    return dot(
        jnp.concatenate([first, second, third, first, second], axis=1), weights[...]
    )


def cross_product(vector, block):
    return dot(
        jnp.concatenate(parts_of(vector, 3), axis=1), jnp.concatenate([block] * 3, axis=0)
    )


def moved(rows, offset):
    return pltpu.roll(rows, (-offset) % rows.shape[0], 0)


def band_apply(bands, spatial):
    result = None
    for matrix in range(2):
        rows = spatial[:, matrix * BLOCK : (matrix + 1) * BLOCK]
        for index, offset in enumerate((0, 1, -1, 2, -2)):
            term = bands[5 * matrix + index] * (moved(rows, offset) if offset else rows)
            result = term if result is None else result + term
    return result


def weights_kernel(
    lists_hbm, pattern_hbm, bands_hbm, right_hbm, obs_hbm, mass_hbm, stiff_hbm,
    bands_ref, flag_ref, diagonal_ref, local_ref, into_ref, out_ref, right_ref, obs_ref,
    lists, pattern, band_rows, right, obs, mass, stiff, arrived,
):
    sources = (lists_hbm, pattern_hbm, bands_hbm, right_hbm, obs_hbm, mass_hbm, stiff_hbm)
    targets = (lists, pattern, band_rows, right, obs, mass, stiff)
    copies = [
        pltpu.make_async_copy(source, target, arrived.at[index])
        for index, (source, target) in enumerate(zip(sources, targets))
    ]
    for copy in copies:
        copy.start()
    for copy in copies[:5]:
        copy.wait()
    time_rows, time_total = right.shape[0], band_rows.shape[2]
    extent = time_rows + 2 * HALO

    first = lax.axis_index("tm") * time_rows - HALO - 2
    tile = (first + time_total) // BLOCK - time_total // BLOCK
    shift = first - tile * BLOCK
    last_tile = time_total // BLOCK - 1
    lane = lax.broadcasted_iota(jnp.int32, (1, BLOCK), 1)
    time = first + lane
    inside = (time >= 0) & (time < time_total)

    def window(band, matrix):
        halves = []
        for index in (tile, tile + 1):
            index = jnp.clip(index, 0, last_tile)
            start = pl.multiple_of(index * BLOCK, BLOCK)
            row = band_rows[band, :, pl.ds(start, BLOCK)][matrix : matrix + 1]
            halves.append(pltpu.roll(row, (BLOCK - shift) % BLOCK, 1))
        line = jnp.where(lane + shift < BLOCK, halves[0], halves[1])
        return jnp.where(inside, line, 0.0)

    lines = []
    for matrix in range(2):
        rows = [window(band, matrix) for band in range(3)]
        for band, offset in TERMS:
            lines.append(pltpu.roll(rows[band], (-(2 + offset)) % BLOCK, 1))
    valid = jnp.where(inside, 1.0, 0.0)
    lines.append(pltpu.roll(valid, BLOCK - 2, 1))
    count = len(lines)
    lines.append(jnp.zeros((BLOCK - count, BLOCK), F32))
    columns = jnp.concatenate(lines, axis=0).T
    for index in range(count):
        bands_ref[index] = jnp.broadcast_to(
            columns[:extent, index : index + 1], (extent, BLOCK)
        )

    entries = lists[0].astype(F32)
    here = lax.broadcasted_iota(jnp.int32, entries.shape, 1) == lax.axis_index("space")
    low = jnp.sum(jnp.where(here, entries, 0.0), axis=1, keepdims=True)
    flag = jnp.broadcast_to(low, (8, BLOCK))
    flag_ref[...] = flag
    swapped = jnp.broadcast_to(low, (BLOCK, BLOCK)) > 0.5
    for ref, source in ((right_ref, right), (obs_ref, obs)):
        one, two = source[:, :BLOCK], source[:, BLOCK:]
        turned = jnp.broadcast_to(low, one.shape) > 0.5
        ref[0] = jnp.where(turned, two, one)
        ref[1] = jnp.where(turned, one, two)
    codes = pattern[...].astype(F32)
    codes = (
        low * codes[1:2] + (1.0 - low) * codes[0:1],
        low * codes[0:1] + (1.0 - low) * codes[1:2],
    )
    own = (low, 1.0 - low)

    for copy in copies[5:]:
        copy.wait()
    eye = lax.broadcasted_iota(jnp.int32, (BLOCK, BLOCK), 0) == lax.broadcasted_iota(
        jnp.int32, (BLOCK, BLOCK), 1
    )
    diagonals = [None] * 4
    for matrix, ref in enumerate((mass, stiff)):

        def block(place, j):
            one, two = ref[place, j].astype(F32), ref[1 - place, j].astype(F32)
            return jnp.where(swapped, two, one)

        stored = [[block(place, j) for j in range(4)] for place in range(2)]
        for place in range(2):
            diagonals[2 * place + matrix] = jnp.sum(
                jnp.where(eye, stored[place][0], 0.0), axis=0, keepdims=True
            )
        for col in range(2):
            lanes = slice((2 * col + matrix) * BLOCK, (2 * col + matrix + 1) * BLOCK)
            for row in range(2):
                total = stored[row][0] if row == col else jnp.zeros((BLOCK, BLOCK), F32)
                for j in (2, 3):
                    named = codes[row][:, j : j + 1] == own[col]
                    total = total + jnp.where(named, 1.0, 0.0) * stored[row][j]
                lead, rest = parts_of(total, 2)
                for k, value in enumerate((lead, lead, lead, rest, rest)):
                    start = (2 * k + row) * BLOCK
                    local_ref[start : start + BLOCK, lanes] = value
        lanes = slice(matrix * BLOCK, (matrix + 1) * BLOCK)
        for place in range(2):
            out_ref[place, :, lanes] = stored[place][1].astype(BF16)
            into_ref[place, :, lanes] = stored[place][1].T.astype(BF16)
    diagonal_ref[...] = jnp.concatenate(diagonals + [jnp.zeros((4, BLOCK), F32)], axis=0)


def stepped(scale, applied, inverse, vector, older):
    result = scale * (inverse * applied - CENTRE * vector)
    return result if older is None else result - older


def prepare_kernel(
    right, obs, before, after, bands, flag, diagonal, local,
    precond_ref, obs_ref, down_ref, up_ref,
):
    swapped = flag[...] > 0.5

    def extended(middle, start):
        ends = []
        for ref in (before, after):
            rows = ref[start : start + HALO]
            one, two = rows[:, :BLOCK], rows[:, BLOCK:]
            ends.append((jnp.where(swapped, two, one), jnp.where(swapped, one, two)))
        return [
            jnp.concatenate([ends[0][k], middle[k], ends[1][k]], axis=0) for k in range(2)
        ]

    rhs, precision = extended(right, 0), extended(obs, HALO)
    valid = bands[10]
    scaled, inverses = [], []
    for place in range(2):
        precond = bands[0] * diagonal[2 * place : 2 * place + 1]
        precond = precond + bands[5] * diagonal[2 * place + 1 : 2 * place + 2]
        precond = precond + precision[place] + (1.0 - valid)
        precond_ref[place] = precond
        obs_ref[place] = precision[place]
        inverses.append(valid / precond)
        scaled.append(rhs[place] * inverses[place])
    spatial = local_product(scaled, local)
    for place, ref in enumerate((down_ref, up_ref)):
        applied = band_apply(bands, spatial[:, 2 * place * BLOCK : 2 * (place + 1) * BLOCK])
        applied = applied + precision[place] * scaled[place]
        ref[0] = scaled[place]
        ref[1] = stepped(1.0 / WIDTH, applied, inverses[place], scaled[place], None)
        ref[2] = inverses[place]


def completed(scale, bands, block, vector, partial, inverse):
    return partial + scale * (inverse * band_apply(bands, cross_product(vector, block)))


def full_step(bands, local, into, vectors, nears, precision, inverses, olders):
    spatial = local_product(vectors, local)
    results = []
    for place in range(2):
        mine = spatial[:, 2 * place * BLOCK : 2 * (place + 1) * BLOCK]
        mine = mine + cross_product(nears[place], into[place])
        applied = band_apply(bands, mine) + precision[place] * vectors[place]
        results.append(
            stepped(2.0 / WIDTH, applied, inverses[place], vectors[place], olders[place])
        )
    return results


def first_kernel(
    down, up, below, above, obs, bands, local, into, out,
    one_ref, down_two_ref, up_two_ref,
):
    own, sides = (down, up), (below, above)
    scale = 1.0 / WIDTH
    inverses = [ref[2] for ref in own]
    vectors = [
        completed(scale, bands, into[k], sides[k][0], own[k][1], inverses[k]) for k in range(2)
    ]
    nears = [
        completed(scale, bands, out[k], own[k][0], sides[k][1], sides[k][2]) for k in range(2)
    ]
    olders = [ref[0] for ref in own]
    two = full_step(bands, local, into, vectors, nears, obs, inverses, olders)
    spatial = local_product(two, local)
    for place, ref in enumerate((down_two_ref, up_two_ref)):
        one_ref[place] = vectors[place]
        applied = band_apply(bands, spatial[:, 2 * place * BLOCK : 2 * (place + 1) * BLOCK])
        applied = applied + obs[place] * two[place]
        ref[0] = two[place]
        ref[1] = stepped(2.0 / WIDTH, applied, inverses[place], two[place], vectors[place])


def second_kernel(
    down, up, below, above, one, down_two, up_two, below_two, above_two, precond, obs,
    bands, local, into, out,
    three_ref, four_ref, sums_ref,
):
    own, sides = (down, up), (below, above)
    own_two, sides_two = (down_two, up_two), (below_two, above_two)
    scale = 2.0 / WIDTH
    inverses = [ref[2] for ref in own]
    vectors = [
        completed(scale, bands, into[k], sides_two[k][0], own_two[k][1], inverses[k])
        for k in range(2)
    ]
    nears = [
        completed(scale, bands, out[k], own_two[k][0], sides_two[k][1], sides[k][2])
        for k in range(2)
    ]
    olders = [ref[0] for ref in own_two]
    four = full_step(bands, local, into, vectors, nears, obs, inverses, olders)
    extent = bands.shape[1]
    inside = slice(HALO, extent - HALO)
    sums = [0.0] * 14
    for place in range(2):
        three_ref[place] = vectors[place]
        four_ref[place] = four[place]
        basis = (own[place][0], one[place], olders[place], vectors[place], four[place])
        basis = [rows[inside] for rows in basis]
        index = 0
        for i in range(4):
            weighted = precond[place][inside] * basis[i]
            for j in range(i, 5):
                term = (weighted * basis[j]).reshape(-1, 8, BLOCK)
                sums[index] = sums[index] + jnp.sum(term, axis=0)
                index += 1
    rows = [jnp.sum(part, axis=0, keepdims=True) for part in sums]
    table = jnp.concatenate(rows + [jnp.zeros((2, BLOCK), F32)], axis=0)
    totals = jnp.sum(table, axis=1, keepdims=True)
    slots = lax.broadcasted_iota(jnp.int32, (16, BLOCK), 0) == lax.broadcasted_iota(
        jnp.int32, (16, BLOCK), 1
    )
    sums_ref[...] = jnp.sum(jnp.where(slots, totals, 0.0), axis=0, keepdims=True)


def added(terms):
    while len(terms) > 1:
        terms = [
            terms[k] + terms[k + 1] if k + 1 < len(terms) else terms[k]
            for k in range(0, len(terms), 2)
        ]
    return terms[0]


def operator(vector, degree):
    result = [[] for _ in range(5)]
    for j in range(degree + 1):
        result[j].append(CENTRE * vector[j])
        if j == 0:
            result[1].append(WIDTH * vector[0])
        else:
            result[j + 1].append((0.5 * WIDTH) * vector[j])
            result[j - 1].append((0.5 * WIDTH) * vector[j])
    return [added(terms) if terms else None for terms in result]


def inner_product(table, left, right):
    terms = []
    for i, a in enumerate(left):
        if a is not None:
            row = [
                table[(min(i, j), max(i, j))] * b for j, b in enumerate(right) if b is not None
            ]
            terms.append(a * added(row))
    return added(terms)


def combined(first, factor, second):
    result = []
    for a, b in zip(first, second):
        if b is None:
            result.append(a)
        else:
            result.append(factor * b if a is None else a + factor * b)
    return result


def final_kernel(
    flag, parts, down, up, one, down_two, up_two, three, four, precond,
    solution_ref, residual_ref,
):
    rows = jnp.sum(parts[...], axis=0, keepdims=True)
    lane = lax.broadcasted_iota(jnp.int32, (1, BLOCK), 1)
    table = {}
    index = 0
    for i in range(4):
        for j in range(i, 5):
            table[(i, j)] = jnp.sum(jnp.where(lane == index, rows, 0.0), axis=1, keepdims=True)
            index += 1
    state = [jnp.ones((1, 1), F32)] + [None] * 4
    direction = list(state)
    answer = [None] * 5
    norm_now = table[(0, 0)]
    for iteration in range(ITERS):
        applied = operator(direction, iteration)
        step = norm_now / inner_product(table, direction, applied)
        answer = combined(answer, step, direction)
        state = combined(state, -step, applied)
        if iteration + 1 < ITERS:
            norm_next = inner_product(table, state, state)
            direction = combined(state, norm_next / norm_now, direction)
            norm_now = norm_next
    swapped = flag[0:1] > 0.5
    inside = slice(HALO, HALO + solution_ref.shape[0])
    solutions, residuals = [], []
    for place, (ref, ref_two) in enumerate(((down, down_two), (up, up_two))):
        basis = (ref[0], one[place], ref_two[0], three[place], four[place])
        basis = [rows[inside] for rows in basis]
        solutions.append(added([answer[k] * basis[k] for k in range(4)]))
        left = added([state[k] * basis[k] for k in range(5)])
        residuals.append(left * precond[place][inside])
    for ref, pair in ((solution_ref, solutions), (residual_ref, residuals)):
        ref[:, :BLOCK] = jnp.where(swapped, pair[1], pair[0])
        ref[:, BLOCK:] = jnp.where(swapped, pair[0], pair[1])


def call(kernel, shapes, *operands, space=VMEM, scratch=(), flops=0):
    return pl.pallas_call(
        kernel,
        out_shape=[
            shape if isinstance(shape, jax.ShapeDtypeStruct) else jax.ShapeDtypeStruct(shape, F32)
            for shape in shapes
        ],
        in_specs=[space] * len(operands),
        out_specs=[VMEM] * len(shapes),
        scratch_shapes=scratch,
        compiler_params=pltpu.CompilerParams(vmem_limit_bytes=32 * 1024 * 1024),
        cost_estimate=pl.CostEstimate(flops=flops, bytes_accessed=1 << 20, transcendentals=0),
    )(*operands)


def ring(axis, wrap):
    devices = lax.axis_size(axis)
    up = [(i, (i + 1) % devices) for i in range(devices if wrap else devices - 1)]
    return up, [(j, i) for i, j in up]


def shards(
    right_side, obs_precision, mass_blocks, stiff_blocks, block_pattern, send_lists, time_bands
):
    time_rows = right_side.shape[0]
    extent = time_rows + 2 * HALO

    up, down = ring("tm", False)
    last = jnp.concatenate([right_side[-HALO:], obs_precision[-HALO:]], axis=0)
    first = jnp.concatenate([right_side[:HALO], obs_precision[:HALO]], axis=0)
    before = lax.ppermute(last, "tm", up)
    after = lax.ppermute(first, "tm", down)

    wide = 2 * BLOCK
    stored = (
        send_lists.transpose(1, 2, 0), block_pattern, time_bands.transpose(1, 0, 2),
        right_side, obs_precision, mass_blocks, stiff_blocks,
    )
    half = (2, time_rows, BLOCK)
    bands, flag, diagonal, local, into, out, right, obs = call(
        weights_kernel,
        [
            (11, extent, BLOCK),
            (8, BLOCK),
            (8, BLOCK),
            jax.ShapeDtypeStruct((5 * wide, 2 * wide), BF16),
            jax.ShapeDtypeStruct((2, BLOCK, wide), BF16),
            jax.ShapeDtypeStruct((2, BLOCK, wide), BF16),
            half,
            half,
        ],
        *[pltpu.with_memory_space_constraint(array, pltpu.HBM) for array in stored],
        space=pl.BlockSpec(memory_space=pltpu.HBM),
        scratch=[pltpu.VMEM(array.shape, array.dtype) for array in stored]
        + [pltpu.SemaphoreType.DMA((len(stored),))],
        flops=1 << 21,
    )

    pair = (2, extent, BLOCK)
    triple = (3, extent, BLOCK)
    precond, precision, to_down, to_up = call(
        prepare_kernel, [pair, pair, triple, triple],
        right, obs, before, after, bands, flag, diagonal, local,
    )
    up, down = ring("space", True)
    below = lax.ppermute(to_up, "space", up)
    above = lax.ppermute(to_down, "space", down)
    one, down_two, up_two = call(
        first_kernel, [pair, pair, pair],
        to_down, to_up, below, above, precision, bands, local, into, out,
    )
    below_two = lax.ppermute(up_two, "space", up)
    above_two = lax.ppermute(down_two, "space", down)
    three, four, sums = call(
        second_kernel, [pair, pair, (1, BLOCK)],
        to_down, to_up, below, above, one, down_two, up_two, below_two, above_two,
        precond, precision, bands, local, into, out,
    )
    for axis in ("space", "tm"):
        devices = lax.axis_size(axis)
        sent = jnp.broadcast_to(sums[None], (devices, 1, BLOCK))
        gathered = lax.all_to_all(sent, axis, 0, 0)
        sums = jnp.sum(gathered, axis=0)
    return tuple(
        call(
            final_kernel, [right_side.shape, right_side.shape],
            flag, sums, to_down, to_up, one, down_two, up_two, three, four, precond,
        )
    )


def solution(mesh):
    placed = (
        P("tm", "space"),
        P("tm", "space"),
        P("space", None, None, None),
        P("space", None, None, None),
        P("space", None),
        P(),
        P(),
    )
    return jax.shard_map(
        shards,
        mesh=mesh,
        in_specs=placed,
        out_specs=(P("tm", "space"), P("tm", "space")),
        check_vma=False,
    )
```

```python
import jax
import jax.numpy as jnp
from jax import lax
from jax.experimental import pallas as pl
from jax.experimental.pallas import tpu as pltpu
from jax.sharding import PartitionSpec as P

ITERS = 4
HALO = 2 * ITERS
FRONT = 2 * HALO
BLOCK = 128
CENTRE = 1.0
WIDTH = 0.6
VMEM = pl.BlockSpec(memory_space=pltpu.VMEM)
F32 = jnp.float32
BF16 = jnp.bfloat16
TERMS = ((0, 0, 0), (1, 1, -1), (-1, 1, 0), (2, 2, -2), (-2, 2, 0))


def parts_of(array, count):
    parts = []
    for _ in range(count):
        part = array.astype(BF16)
        parts.append(part)
        array = array - part.astype(F32)
    return parts


def dot(left, right):
    return jnp.dot(left, right, preferred_element_type=F32)


def local_product(vectors, weights):
    first, second, third = parts_of(jnp.concatenate(vectors, axis=1), 3)
    return dot(jnp.concatenate([first, second, third, first], axis=1), weights[...])


def cross_product(vector, block):
    return dot(
        jnp.concatenate(parts_of(vector, 3), axis=1), jnp.concatenate([block] * 3, axis=0)
    )


def moved(rows, offset):
    return pltpu.roll(rows, (-offset) % rows.shape[0], 0)


def band_apply(bands, spatial):
    first, second = spatial[:, :BLOCK], spatial[:, BLOCK:]
    result = None
    for index, (offset, _, _) in enumerate(TERMS):
        term = bands[index] * first + bands[5 + index] * second
        if offset:
            term = moved(term, offset)
        result = term if result is None else result + term
    return result


def weights_kernel(
    lists_hbm, pattern_hbm, bands_hbm, right_hbm, obs_hbm, mass_hbm, stiff_hbm,
    bands_ref, flag_ref, diagonal_ref, local_ref, into_ref, out_ref, right_ref, obs_ref,
    lists, pattern, band_rows, right, obs, mass, stiff, arrived,
):
    sources = (lists_hbm, pattern_hbm, bands_hbm, right_hbm, obs_hbm, mass_hbm, stiff_hbm)
    targets = (lists, pattern, band_rows, right, obs, mass, stiff)
    copies = [
        pltpu.make_async_copy(source, target, arrived.at[index])
        for index, (source, target) in enumerate(zip(sources, targets))
    ]
    for copy in copies:
        copy.start()
    for copy in copies[:5]:
        copy.wait()
    time_rows, time_total = right.shape[0], band_rows.shape[2]
    extent = time_rows + FRONT

    first = lax.axis_index("tm") * time_rows - FRONT - 2
    tile = (first + time_total) // BLOCK - time_total // BLOCK
    shift = first - tile * BLOCK
    last_tile = time_total // BLOCK - 1
    lane = lax.broadcasted_iota(jnp.int32, (1, BLOCK), 1)
    time = first + lane
    inside = (time >= 0) & (time < time_total)

    def window(band, matrix):
        halves = []
        for index in (tile, tile + 1):
            index = jnp.clip(index, 0, last_tile)
            start = pl.multiple_of(index * BLOCK, BLOCK)
            row = band_rows[band, :, pl.ds(start, BLOCK)][matrix : matrix + 1]
            halves.append(pltpu.roll(row, (BLOCK - shift) % BLOCK, 1))
        line = jnp.where(lane + shift < BLOCK, halves[0], halves[1])
        return jnp.where(inside, line, 0.0)

    lines = []
    for matrix in range(2):
        rows = [window(band, matrix) for band in range(3)]
        for offset, band, shifted in TERMS:
            line = pltpu.roll(rows[band], (-(2 + shifted)) % BLOCK, 1)
            lines.append(jnp.where(lane >= offset, line, 0.0) if offset > 0 else line)
    valid = jnp.where(inside, 1.0, 0.0)
    lines.append(pltpu.roll(valid, BLOCK - 2, 1))
    count = len(lines)
    lines.append(jnp.zeros((BLOCK - count, BLOCK), F32))
    columns = jnp.concatenate(lines, axis=0).T
    for index in range(count):
        bands_ref[index] = jnp.broadcast_to(
            columns[:extent, index : index + 1], (extent, BLOCK)
        )

    entries = lists[0].astype(F32)
    here = lax.broadcasted_iota(jnp.int32, entries.shape, 1) == lax.axis_index("space")
    low = jnp.sum(jnp.where(here, entries, 0.0), axis=1, keepdims=True)
    flag = jnp.broadcast_to(low, (8, BLOCK))
    flag_ref[...] = flag
    swapped = jnp.broadcast_to(low, (BLOCK, BLOCK)) > 0.5
    for ref, source in ((right_ref, right), (obs_ref, obs)):
        one, two = source[:, :BLOCK], source[:, BLOCK:]
        turned = jnp.broadcast_to(low, one.shape) > 0.5
        ref[0] = jnp.where(turned, two, one)
        ref[1] = jnp.where(turned, one, two)
    codes = pattern[...].astype(F32)
    codes = (
        low * codes[1:2] + (1.0 - low) * codes[0:1],
        low * codes[0:1] + (1.0 - low) * codes[1:2],
    )
    own = (low, 1.0 - low)

    for copy in copies[5:]:
        copy.wait()
    eye = lax.broadcasted_iota(jnp.int32, (BLOCK, BLOCK), 0) == lax.broadcasted_iota(
        jnp.int32, (BLOCK, BLOCK), 1
    )
    diagonals = [None] * 4
    for matrix, ref in enumerate((mass, stiff)):

        def block(place, j):
            one, two = ref[place, j].astype(F32), ref[1 - place, j].astype(F32)
            return jnp.where(swapped, two, one)

        stored = [[block(place, j) for j in range(4)] for place in range(2)]
        for place in range(2):
            diagonals[2 * place + matrix] = jnp.sum(
                jnp.where(eye, stored[place][0], 0.0), axis=0, keepdims=True
            )
        for col in range(2):
            lanes = slice((2 * col + matrix) * BLOCK, (2 * col + matrix + 1) * BLOCK)
            for row in range(2):
                total = stored[row][0] if row == col else jnp.zeros((BLOCK, BLOCK), F32)
                for j in (2, 3):
                    named = codes[row][:, j : j + 1] == own[col]
                    total = total + jnp.where(named, 1.0, 0.0) * stored[row][j]
                lead, rest = parts_of(total, 2)
                for k, value in enumerate((lead, lead, lead, rest)):
                    start = (2 * k + row) * BLOCK
                    local_ref[start : start + BLOCK, lanes] = value
        lanes = slice(matrix * BLOCK, (matrix + 1) * BLOCK)
        for place in range(2):
            out_ref[place, :, lanes] = stored[place][1].astype(BF16)
            into_ref[place, :, lanes] = stored[place][1].T.astype(BF16)
    diagonal_ref[...] = jnp.concatenate(diagonals + [jnp.zeros((4, BLOCK), F32)], axis=0)


def stepped(scale, applied, inverse, vector, older):
    result = scale * (inverse * applied - CENTRE * vector)
    return result if older is None else result - older


def prepare_kernel(
    right, obs, before, bands, flag, diagonal, local,
    precond_ref, obs_ref, down_ref, up_ref,
):
    swapped = flag[...] > 0.5

    def extended(middle, start):
        rows = before[start : start + FRONT]
        one, two = rows[:, :BLOCK], rows[:, BLOCK:]
        turned = jnp.concatenate([swapped] * (FRONT // 8), axis=0)
        ends = (jnp.where(turned, two, one), jnp.where(turned, one, two))
        return [jnp.concatenate([ends[k], middle[k]], axis=0) for k in range(2)]

    rhs, precision = extended(right, 0), extended(obs, FRONT)
    valid = bands[10]
    scaled, inverses = [], []
    for place in range(2):
        precond = bands[0] * diagonal[2 * place : 2 * place + 1]
        precond = precond + bands[5] * diagonal[2 * place + 1 : 2 * place + 2]
        precond = precond + precision[place] + (1.0 - valid)
        precond_ref[place] = precond
        obs_ref[place] = precision[place]
        inverses.append(valid / precond)
        scaled.append(rhs[place] * inverses[place])
    spatial = local_product(scaled, local)
    for place, ref in enumerate((down_ref, up_ref)):
        applied = band_apply(bands, spatial[:, 2 * place * BLOCK : 2 * (place + 1) * BLOCK])
        applied = applied + precision[place] * scaled[place]
        ref[0] = scaled[place]
        ref[1] = stepped(1.0 / WIDTH, applied, inverses[place], scaled[place], None)
        ref[2] = inverses[place]


def completed(scale, bands, block, vector, partial, inverse):
    return partial + scale * (inverse * band_apply(bands, cross_product(vector, block)))


def full_step(bands, local, into, vectors, nears, precision, inverses, olders):
    spatial = local_product(vectors, local)
    results = []
    for place in range(2):
        mine = spatial[:, 2 * place * BLOCK : 2 * (place + 1) * BLOCK]
        mine = mine + cross_product(nears[place], into[place])
        applied = band_apply(bands, mine) + precision[place] * vectors[place]
        results.append(
            stepped(2.0 / WIDTH, applied, inverses[place], vectors[place], olders[place])
        )
    return results


def first_kernel(
    down, up, below, above, obs, bands, local, into, out,
    one_ref, down_two_ref, up_two_ref,
):
    own, sides = (down, up), (below, above)
    scale = 1.0 / WIDTH
    inverses = [ref[2] for ref in own]
    vectors = [
        completed(scale, bands, into[k], sides[k][0], own[k][1], inverses[k]) for k in range(2)
    ]
    nears = [
        completed(scale, bands, out[k], own[k][0], sides[k][1], sides[k][2]) for k in range(2)
    ]
    olders = [ref[0] for ref in own]
    two = full_step(bands, local, into, vectors, nears, obs, inverses, olders)
    spatial = local_product(two, local)
    for place, ref in enumerate((down_two_ref, up_two_ref)):
        one_ref[place] = vectors[place]
        applied = band_apply(bands, spatial[:, 2 * place * BLOCK : 2 * (place + 1) * BLOCK])
        applied = applied + obs[place] * two[place]
        ref[0] = two[place]
        ref[1] = stepped(2.0 / WIDTH, applied, inverses[place], two[place], vectors[place])


def second_kernel(
    down, up, below, above, one, down_two, up_two, below_two, above_two, precond, obs,
    bands, local, into, out,
    three_ref, four_ref, back_ref, sums_ref,
):
    own, sides = (down, up), (below, above)
    own_two, sides_two = (down_two, up_two), (below_two, above_two)
    scale = 2.0 / WIDTH
    inverses = [ref[2] for ref in own]
    vectors = [
        completed(scale, bands, into[k], sides_two[k][0], own_two[k][1], inverses[k])
        for k in range(2)
    ]
    nears = [
        completed(scale, bands, out[k], own_two[k][0], sides_two[k][1], sides[k][2])
        for k in range(2)
    ]
    olders = [ref[0] for ref in own_two]
    four = full_step(bands, local, into, vectors, nears, obs, inverses, olders)
    extent = bands.shape[1]
    final = lax.axis_index("tm") == lax.axis_size("tm") - 1
    counted = lax.broadcasted_iota(jnp.int32, (extent - HALO, BLOCK), 0) < extent - FRONT
    counted = jnp.where(counted | final, 1.0, 0.0)
    sums = [0.0] * 14
    for place in range(2):
        three_ref[place] = vectors[place]
        four_ref[place] = four[place]
        basis = (own[place][0], one[place], olders[place], vectors[place], four[place])
        for k in range(4):
            back_ref[place, k] = basis[k + 1][HALO:FRONT]
        basis = [rows[HALO:] for rows in basis]
        weight = counted * precond[place][HALO:]
        index = 0
        for i in range(4):
            weighted = weight * basis[i]
            for j in range(i, 5):
                term = (weighted * basis[j]).reshape(-1, 8, BLOCK)
                sums[index] = sums[index] + jnp.sum(term, axis=0)
                index += 1
    rows = [jnp.sum(part, axis=0, keepdims=True) for part in sums]
    table = jnp.concatenate(rows + [jnp.zeros((2, BLOCK), F32)], axis=0)
    totals = jnp.sum(table, axis=1, keepdims=True)
    slots = lax.broadcasted_iota(jnp.int32, (16, BLOCK), 0) == lax.broadcasted_iota(
        jnp.int32, (16, BLOCK), 1
    )
    sums_ref[...] = jnp.sum(jnp.where(slots, totals, 0.0), axis=0, keepdims=True)


def added(terms):
    while len(terms) > 1:
        terms = [
            terms[k] + terms[k + 1] if k + 1 < len(terms) else terms[k]
            for k in range(0, len(terms), 2)
        ]
    return terms[0]


def operator(vector, degree):
    result = [[] for _ in range(5)]
    for j in range(degree + 1):
        result[j].append(CENTRE * vector[j])
        if j == 0:
            result[1].append(WIDTH * vector[0])
        else:
            result[j + 1].append((0.5 * WIDTH) * vector[j])
            result[j - 1].append((0.5 * WIDTH) * vector[j])
    return [added(terms) if terms else None for terms in result]


def inner_product(table, left, right):
    terms = []
    for i, a in enumerate(left):
        if a is not None:
            row = [
                table[(min(i, j), max(i, j))] * b for j, b in enumerate(right) if b is not None
            ]
            terms.append(a * added(row))
    return added(terms)


def combined(first, factor, second):
    result = []
    for a, b in zip(first, second):
        if b is None:
            result.append(a)
        else:
            result.append(factor * b if a is None else a + factor * b)
    return result


def final_kernel(
    flag, parts, down, up, one, down_two, up_two, three, four, precond, back,
    solution_ref, residual_ref,
):
    rows = jnp.sum(parts[...], axis=0, keepdims=True)
    lane = lax.broadcasted_iota(jnp.int32, (1, BLOCK), 1)
    table = {}
    index = 0
    for i in range(4):
        for j in range(i, 5):
            table[(i, j)] = jnp.sum(jnp.where(lane == index, rows, 0.0), axis=1, keepdims=True)
            index += 1
    state = [jnp.ones((1, 1), F32)] + [None] * 4
    direction = list(state)
    answer = [None] * 5
    norm_now = table[(0, 0)]
    for iteration in range(ITERS):
        applied = operator(direction, iteration)
        step = norm_now / inner_product(table, direction, applied)
        answer = combined(answer, step, direction)
        state = combined(state, -step, applied)
        if iteration + 1 < ITERS:
            norm_next = inner_product(table, state, state)
            direction = combined(state, norm_next / norm_now, direction)
            norm_now = norm_next
    swapped = flag[0:1] > 0.5
    final = lax.axis_index("tm") == lax.axis_size("tm") - 1
    solutions, residuals = [], []
    for place, (ref, ref_two) in enumerate(((down, down_two), (up, up_two))):
        basis = (ref[0], one[place], ref_two[0], three[place], four[place])
        extent = precond.shape[1]
        start = basis[0][FRONT:]
        basis = [
            jnp.concatenate(
                [
                    rows[FRONT : extent - HALO],
                    jnp.where(final, rows[extent - HALO :], back[place, k]),
                ],
                axis=0,
            )
            for k, rows in enumerate(basis[1:])
        ]
        basis.insert(0, start)
        solutions.append(added([answer[k] * basis[k] for k in range(4)]))
        left = added([state[k] * basis[k] for k in range(5)])
        residuals.append(left * precond[place][FRONT:])
    for ref, pair in ((solution_ref, solutions), (residual_ref, residuals)):
        ref[:, :BLOCK] = jnp.where(swapped, pair[1], pair[0])
        ref[:, BLOCK:] = jnp.where(swapped, pair[0], pair[1])


def call(kernel, shapes, *operands, space=VMEM, scratch=(), flops=0):
    return pl.pallas_call(
        kernel,
        out_shape=[
            shape if isinstance(shape, jax.ShapeDtypeStruct) else jax.ShapeDtypeStruct(shape, F32)
            for shape in shapes
        ],
        in_specs=[space] * len(operands),
        out_specs=[VMEM] * len(shapes),
        scratch_shapes=scratch,
        compiler_params=pltpu.CompilerParams(vmem_limit_bytes=32 * 1024 * 1024),
        cost_estimate=pl.CostEstimate(flops=flops, bytes_accessed=1 << 20, transcendentals=0),
    )(*operands)


def ring(axis, wrap):
    devices = lax.axis_size(axis)
    up = [(i, (i + 1) % devices) for i in range(devices if wrap else devices - 1)]
    return up, [(j, i) for i, j in up]


def shards(
    right_side, obs_precision, mass_blocks, stiff_blocks, block_pattern, send_lists, time_bands
):
    time_rows = right_side.shape[0]
    extent = time_rows + FRONT

    later, earlier = ring("tm", False)
    last = jnp.concatenate([right_side[-FRONT:], obs_precision[-FRONT:]], axis=0)
    before = lax.ppermute(last, "tm", later)

    wide = 2 * BLOCK
    stored = (
        send_lists.transpose(1, 2, 0), block_pattern, time_bands.transpose(1, 0, 2),
        right_side, obs_precision, mass_blocks, stiff_blocks,
    )
    half = (2, time_rows, BLOCK)
    bands, flag, diagonal, local, into, out, right, obs = call(
        weights_kernel,
        [
            (11, extent, BLOCK),
            (8, BLOCK),
            (8, BLOCK),
            jax.ShapeDtypeStruct((4 * wide, 2 * wide), BF16),
            jax.ShapeDtypeStruct((2, BLOCK, wide), BF16),
            jax.ShapeDtypeStruct((2, BLOCK, wide), BF16),
            half,
            half,
        ],
        *[pltpu.with_memory_space_constraint(array, pltpu.HBM) for array in stored],
        space=pl.BlockSpec(memory_space=pltpu.HBM),
        scratch=[pltpu.VMEM(array.shape, array.dtype) for array in stored]
        + [pltpu.SemaphoreType.DMA((len(stored),))],
        flops=1 << 21,
    )

    pair = (2, extent, BLOCK)
    triple = (3, extent, BLOCK)
    precond, precision, to_down, to_up = call(
        prepare_kernel, [pair, pair, triple, triple],
        right, obs, before, bands, flag, diagonal, local,
    )
    up, down = ring("space", True)
    below = lax.ppermute(to_up, "space", up)
    above = lax.ppermute(to_down, "space", down)
    one, down_two, up_two = call(
        first_kernel, [pair, pair, pair],
        to_down, to_up, below, above, precision, bands, local, into, out,
    )
    below_two = lax.ppermute(up_two, "space", up)
    above_two = lax.ppermute(down_two, "space", down)
    three, four, back, sums = call(
        second_kernel, [pair, pair, (2, 4, HALO, BLOCK), (1, BLOCK)],
        to_down, to_up, below, above, one, down_two, up_two, below_two, above_two,
        precond, precision, bands, local, into, out,
    )
    back = lax.ppermute(back, "tm", earlier)
    for axis in ("space", "tm"):
        devices = lax.axis_size(axis)
        sent = jnp.broadcast_to(sums[None], (devices, 1, BLOCK))
        gathered = lax.all_to_all(sent, axis, 0, 0)
        sums = jnp.sum(gathered, axis=0)
    return tuple(
        call(
            final_kernel, [right_side.shape, right_side.shape],
            flag, sums, to_down, to_up, one, down_two, up_two, three, four, precond, back,
        )
    )


def solution(mesh):
    placed = (
        P("tm", "space"),
        P("tm", "space"),
        P("space", None, None, None),
        P("space", None, None, None),
        P("space", None),
        P(),
        P(),
    )
    return jax.shard_map(
        shards,
        mesh=mesh,
        in_specs=placed,
        out_specs=(P("tm", "space"), P("tm", "space")),
        check_vma=False,
    )
```

```python
import jax
import jax.numpy as jnp
from jax import lax
from jax.experimental import pallas as pl
from jax.experimental.pallas import tpu as pltpu
from jax.sharding import PartitionSpec as P

ITERS = 4
HALO = 2 * ITERS
FRONT = 2 * HALO
BLOCK = 128
CENTRE = 1.0
WIDTH = 0.6
VMEM = pl.BlockSpec(memory_space=pltpu.VMEM)
F32 = jnp.float32
BF16 = jnp.bfloat16
TERMS = ((0, 0, 0), (1, 1, -1), (-1, 1, 0), (2, 2, -2), (-2, 2, 0))


def parts_of(array, count):
    parts = []
    for _ in range(count):
        part = array.astype(BF16)
        parts.append(part)
        array = array - part.astype(F32)
    return parts


def dot(left, right):
    return jnp.dot(left, right, preferred_element_type=F32)


def stacked_product(parts, block):
    rows = parts[0].shape[0]
    product = dot(jnp.concatenate(parts, axis=0), block)
    result = product[:rows]
    for k in range(1, len(parts)):
        result = result + product[k * rows : (k + 1) * rows]
    return result


def local_product(vectors, weights):
    parts = parts_of(jnp.concatenate(vectors, axis=1), 3)
    return stacked_product(parts, weights[0]) + dot(parts[0], weights[1])


def cross_product(vector, block):
    return stacked_product(parts_of(vector, 3), block)


def moved(rows, offset):
    return pltpu.roll(rows, (-offset) % rows.shape[0], 0)


def band_apply(bands, spatial):
    first, second = spatial[:, :BLOCK], spatial[:, BLOCK:]
    result = None
    for index, (offset, _, _) in enumerate(TERMS):
        term = bands[index] * first + bands[5 + index] * second
        if offset:
            term = moved(term, offset)
        result = term if result is None else result + term
    return result


def weights_kernel(
    lists_hbm, pattern_hbm, bands_hbm, right_hbm, obs_hbm, mass_hbm, stiff_hbm,
    bands_ref, flag_ref, diagonal_ref, local_ref, into_ref, out_ref, right_ref, obs_ref,
    lists, pattern, band_rows, right, obs, mass, stiff, arrived,
):
    sources = (lists_hbm, pattern_hbm, bands_hbm, right_hbm, obs_hbm, mass_hbm, stiff_hbm)
    targets = (lists, pattern, band_rows, right, obs, mass, stiff)
    copies = [
        pltpu.make_async_copy(source, target, arrived.at[index])
        for index, (source, target) in enumerate(zip(sources, targets))
    ]
    for copy in copies:
        copy.start()
    for copy in copies[:5]:
        copy.wait()
    time_rows, time_total = right.shape[0], band_rows.shape[2]
    extent = time_rows + FRONT

    first = lax.axis_index("tm") * time_rows - FRONT - 2
    tile = (first + time_total) // BLOCK - time_total // BLOCK
    shift = first - tile * BLOCK
    last_tile = time_total // BLOCK - 1
    lane = lax.broadcasted_iota(jnp.int32, (1, BLOCK), 1)
    time = first + lane
    inside = (time >= 0) & (time < time_total)

    def window(band, matrix):
        halves = []
        for index in (tile, tile + 1):
            index = jnp.clip(index, 0, last_tile)
            start = pl.multiple_of(index * BLOCK, BLOCK)
            row = band_rows[band, :, pl.ds(start, BLOCK)][matrix : matrix + 1]
            halves.append(pltpu.roll(row, (BLOCK - shift) % BLOCK, 1))
        line = jnp.where(lane + shift < BLOCK, halves[0], halves[1])
        return jnp.where(inside, line, 0.0)

    lines = []
    for matrix in range(2):
        rows = [window(band, matrix) for band in range(3)]
        for offset, band, shifted in TERMS:
            line = pltpu.roll(rows[band], (-(2 + shifted)) % BLOCK, 1)
            lines.append(jnp.where(lane >= offset, line, 0.0) if offset > 0 else line)
    valid = jnp.where(inside, 1.0, 0.0)
    lines.append(pltpu.roll(valid, BLOCK - 2, 1))
    count = len(lines)
    lines.append(jnp.zeros((BLOCK - count, BLOCK), F32))
    columns = jnp.concatenate(lines, axis=0).T
    for index in range(count):
        bands_ref[index] = jnp.broadcast_to(
            columns[:extent, index : index + 1], (extent, BLOCK)
        )

    entries = lists[0].astype(F32)
    here = lax.broadcasted_iota(jnp.int32, entries.shape, 1) == lax.axis_index("space")
    low = jnp.sum(jnp.where(here, entries, 0.0), axis=1, keepdims=True)
    flag = jnp.broadcast_to(low, (8, BLOCK))
    flag_ref[...] = flag
    swapped = jnp.broadcast_to(low, (BLOCK, BLOCK)) > 0.5
    for ref, source in ((right_ref, right), (obs_ref, obs)):
        one, two = source[:, :BLOCK], source[:, BLOCK:]
        turned = jnp.broadcast_to(low, one.shape) > 0.5
        ref[0] = jnp.where(turned, two, one)
        ref[1] = jnp.where(turned, one, two)
    codes = pattern[...].astype(F32)
    codes = (
        low * codes[1:2] + (1.0 - low) * codes[0:1],
        low * codes[0:1] + (1.0 - low) * codes[1:2],
    )
    own = (low, 1.0 - low)

    for copy in copies[5:]:
        copy.wait()
    eye = lax.broadcasted_iota(jnp.int32, (BLOCK, BLOCK), 0) == lax.broadcasted_iota(
        jnp.int32, (BLOCK, BLOCK), 1
    )
    diagonals = [None] * 4
    for matrix, ref in enumerate((mass, stiff)):

        def block(place, j):
            one, two = ref[place, j].astype(F32), ref[1 - place, j].astype(F32)
            return jnp.where(swapped, two, one)

        stored = [[block(place, j) for j in range(4)] for place in range(2)]
        for place in range(2):
            diagonals[2 * place + matrix] = jnp.sum(
                jnp.where(eye, stored[place][0], 0.0), axis=0, keepdims=True
            )
        for col in range(2):
            lanes = slice((2 * col + matrix) * BLOCK, (2 * col + matrix + 1) * BLOCK)
            for row in range(2):
                total = stored[row][0] if row == col else jnp.zeros((BLOCK, BLOCK), F32)
                for j in (2, 3):
                    named = codes[row][:, j : j + 1] == own[col]
                    total = total + jnp.where(named, 1.0, 0.0) * stored[row][j]
                lead, rest = parts_of(total, 2)
                for k, value in enumerate((lead, rest)):
                    local_ref[k, row * BLOCK : (row + 1) * BLOCK, lanes] = value
        lanes = slice(matrix * BLOCK, (matrix + 1) * BLOCK)
        for place in range(2):
            out_ref[place, :, lanes] = stored[place][1].astype(BF16)
            into_ref[place, :, lanes] = stored[place][1].T.astype(BF16)
    diagonal_ref[...] = jnp.concatenate(diagonals + [jnp.zeros((4, BLOCK), F32)], axis=0)


def stepped(scale, applied, inverse, vector, older):
    result = scale * (inverse * applied - CENTRE * vector)
    return result if older is None else result - older


def prepare_kernel(
    right, obs, before, bands, flag, diagonal, local,
    precond_ref, obs_ref, down_ref, up_ref,
):
    swapped = flag[...] > 0.5

    def extended(middle, start):
        rows = before[start : start + FRONT]
        one, two = rows[:, :BLOCK], rows[:, BLOCK:]
        turned = jnp.concatenate([swapped] * (FRONT // 8), axis=0)
        ends = (jnp.where(turned, two, one), jnp.where(turned, one, two))
        return [jnp.concatenate([ends[k], middle[k]], axis=0) for k in range(2)]

    rhs, precision = extended(right, 0), extended(obs, FRONT)
    valid = bands[10]
    scaled, inverses = [], []
    for place in range(2):
        precond = bands[0] * diagonal[2 * place : 2 * place + 1]
        precond = precond + bands[5] * diagonal[2 * place + 1 : 2 * place + 2]
        precond = precond + precision[place] + (1.0 - valid)
        precond_ref[place] = precond
        obs_ref[place] = precision[place]
        inverses.append(valid / precond)
        scaled.append(rhs[place] * inverses[place])
    spatial = local_product(scaled, local)
    for place, ref in enumerate((down_ref, up_ref)):
        applied = band_apply(bands, spatial[:, 2 * place * BLOCK : 2 * (place + 1) * BLOCK])
        applied = applied + precision[place] * scaled[place]
        ref[0] = scaled[place]
        ref[1] = stepped(1.0 / WIDTH, applied, inverses[place], scaled[place], None)
        ref[2] = inverses[place]


def completed(scale, bands, block, vector, partial, inverse):
    return partial + scale * (inverse * band_apply(bands, cross_product(vector, block)))


def full_step(bands, local, into, vectors, nears, precision, inverses, olders):
    spatial = local_product(vectors, local)
    results = []
    for place in range(2):
        mine = spatial[:, 2 * place * BLOCK : 2 * (place + 1) * BLOCK]
        mine = mine + cross_product(nears[place], into[place])
        applied = band_apply(bands, mine) + precision[place] * vectors[place]
        results.append(
            stepped(2.0 / WIDTH, applied, inverses[place], vectors[place], olders[place])
        )
    return results


def first_kernel(
    down, up, below, above, obs, bands, local, into, out,
    one_ref, down_two_ref, up_two_ref,
):
    own, sides = (down, up), (below, above)
    scale = 1.0 / WIDTH
    inverses = [ref[2] for ref in own]
    vectors = [
        completed(scale, bands, into[k], sides[k][0], own[k][1], inverses[k]) for k in range(2)
    ]
    nears = [
        completed(scale, bands, out[k], own[k][0], sides[k][1], sides[k][2]) for k in range(2)
    ]
    olders = [ref[0] for ref in own]
    two = full_step(bands, local, into, vectors, nears, obs, inverses, olders)
    spatial = local_product(two, local)
    for place, ref in enumerate((down_two_ref, up_two_ref)):
        one_ref[place] = vectors[place]
        applied = band_apply(bands, spatial[:, 2 * place * BLOCK : 2 * (place + 1) * BLOCK])
        applied = applied + obs[place] * two[place]
        ref[0] = two[place]
        ref[1] = stepped(2.0 / WIDTH, applied, inverses[place], two[place], vectors[place])


def second_kernel(
    down, up, below, above, one, down_two, up_two, below_two, above_two, precond, obs,
    bands, local, into, out,
    three_ref, four_ref, back_ref, sums_ref,
):
    own, sides = (down, up), (below, above)
    own_two, sides_two = (down_two, up_two), (below_two, above_two)
    scale = 2.0 / WIDTH
    inverses = [ref[2] for ref in own]
    vectors = [
        completed(scale, bands, into[k], sides_two[k][0], own_two[k][1], inverses[k])
        for k in range(2)
    ]
    nears = [
        completed(scale, bands, out[k], own_two[k][0], sides_two[k][1], sides[k][2])
        for k in range(2)
    ]
    olders = [ref[0] for ref in own_two]
    four = full_step(bands, local, into, vectors, nears, obs, inverses, olders)
    extent = bands.shape[1]
    final = lax.axis_index("tm") == lax.axis_size("tm") - 1
    counted = lax.broadcasted_iota(jnp.int32, (extent - HALO, BLOCK), 0) < extent - FRONT
    counted = jnp.where(counted | final, 1.0, 0.0)
    sums = [0.0] * 14
    for place in range(2):
        three_ref[place] = vectors[place]
        four_ref[place] = four[place]
        basis = (own[place][0], one[place], olders[place], vectors[place], four[place])
        for k in range(4):
            back_ref[place, k] = basis[k + 1][HALO:FRONT]
        basis = [rows[HALO:] for rows in basis]
        weight = counted * precond[place][HALO:]
        index = 0
        for i in range(4):
            weighted = weight * basis[i]
            for j in range(i, 5):
                term = (weighted * basis[j]).reshape(-1, 8, BLOCK)
                sums[index] = sums[index] + jnp.sum(term, axis=0)
                index += 1
    rows = [jnp.sum(part, axis=0, keepdims=True) for part in sums]
    table = jnp.concatenate(rows + [jnp.zeros((2, BLOCK), F32)], axis=0)
    totals = jnp.sum(table, axis=1, keepdims=True)
    slots = lax.broadcasted_iota(jnp.int32, (16, BLOCK), 0) == lax.broadcasted_iota(
        jnp.int32, (16, BLOCK), 1
    )
    line = jnp.sum(jnp.where(slots, totals, 0.0), axis=0, keepdims=True)
    sums_ref[...] = jnp.broadcast_to(line[None], sums_ref.shape)


def added(terms):
    while len(terms) > 1:
        terms = [
            terms[k] + terms[k + 1] if k + 1 < len(terms) else terms[k]
            for k in range(0, len(terms), 2)
        ]
    return terms[0]


def operator(vector, degree):
    result = [[] for _ in range(5)]
    for j in range(degree + 1):
        result[j].append(CENTRE * vector[j])
        if j == 0:
            result[1].append(WIDTH * vector[0])
        else:
            result[j + 1].append((0.5 * WIDTH) * vector[j])
            result[j - 1].append((0.5 * WIDTH) * vector[j])
    return [added(terms) if terms else None for terms in result]


def inner_product(table, left, right):
    terms = []
    for i, a in enumerate(left):
        if a is not None:
            row = [
                table[(min(i, j), max(i, j))] * b for j, b in enumerate(right) if b is not None
            ]
            terms.append(a * added(row))
    return added(terms)


def combined(first, factor, second):
    result = []
    for a, b in zip(first, second):
        if b is None:
            result.append(a)
        else:
            result.append(factor * b if a is None else a + factor * b)
    return result


def final_kernel(
    flag, parts, down, up, one, down_two, up_two, three, four, precond, back,
    solution_ref, residual_ref,
):
    rows = jnp.sum(parts[...], axis=0, keepdims=True)
    lane = lax.broadcasted_iota(jnp.int32, (1, BLOCK), 1)
    table = {}
    index = 0
    for i in range(4):
        for j in range(i, 5):
            table[(i, j)] = jnp.sum(jnp.where(lane == index, rows, 0.0), axis=1, keepdims=True)
            index += 1
    state = [jnp.ones((1, 1), F32)] + [None] * 4
    direction = list(state)
    answer = [None] * 5
    norm_now = table[(0, 0)]
    for iteration in range(ITERS):
        applied = operator(direction, iteration)
        step = norm_now / inner_product(table, direction, applied)
        answer = combined(answer, step, direction)
        state = combined(state, -step, applied)
        if iteration + 1 < ITERS:
            norm_next = inner_product(table, state, state)
            direction = combined(state, norm_next / norm_now, direction)
            norm_now = norm_next
    swapped = flag[0:1] > 0.5
    final = lax.axis_index("tm") == lax.axis_size("tm") - 1
    solutions, residuals = [], []
    for place, (ref, ref_two) in enumerate(((down, down_two), (up, up_two))):
        basis = (ref[0], one[place], ref_two[0], three[place], four[place])
        extent = precond.shape[1]
        start = basis[0][FRONT:]
        basis = [
            jnp.concatenate(
                [
                    rows[FRONT : extent - HALO],
                    jnp.where(final, rows[extent - HALO :], back[place, k]),
                ],
                axis=0,
            )
            for k, rows in enumerate(basis[1:])
        ]
        basis.insert(0, start)
        solutions.append(added([answer[k] * basis[k] for k in range(4)]))
        left = added([state[k] * basis[k] for k in range(5)])
        residuals.append(left * precond[place][FRONT:])
    for ref, pair in ((solution_ref, solutions), (residual_ref, residuals)):
        ref[:, :BLOCK] = jnp.where(swapped, pair[1], pair[0])
        ref[:, BLOCK:] = jnp.where(swapped, pair[0], pair[1])


def call(kernel, shapes, *operands, space=VMEM, scratch=(), flops=0):
    return pl.pallas_call(
        kernel,
        out_shape=[
            shape if isinstance(shape, jax.ShapeDtypeStruct) else jax.ShapeDtypeStruct(shape, F32)
            for shape in shapes
        ],
        in_specs=[space] * len(operands),
        out_specs=[VMEM] * len(shapes),
        scratch_shapes=scratch,
        compiler_params=pltpu.CompilerParams(vmem_limit_bytes=32 * 1024 * 1024),
        cost_estimate=pl.CostEstimate(flops=flops, bytes_accessed=1 << 20, transcendentals=0),
    )(*operands)


def ring(axis, wrap):
    devices = lax.axis_size(axis)
    up = [(i, (i + 1) % devices) for i in range(devices if wrap else devices - 1)]
    return up, [(j, i) for i, j in up]


def shards(
    right_side, obs_precision, mass_blocks, stiff_blocks, block_pattern, send_lists, time_bands
):
    time_rows = right_side.shape[0]
    extent = time_rows + FRONT

    later, earlier = ring("tm", False)
    last = jnp.concatenate([right_side[-FRONT:], obs_precision[-FRONT:]], axis=0)
    before = lax.ppermute(last, "tm", later)

    wide = 2 * BLOCK
    stored = (
        send_lists.transpose(1, 2, 0), block_pattern, time_bands.transpose(1, 0, 2),
        right_side, obs_precision, mass_blocks, stiff_blocks,
    )
    half = (2, time_rows, BLOCK)
    bands, flag, diagonal, local, into, out, right, obs = call(
        weights_kernel,
        [
            (11, extent, BLOCK),
            (8, BLOCK),
            (8, BLOCK),
            jax.ShapeDtypeStruct((2, wide, 2 * wide), BF16),
            jax.ShapeDtypeStruct((2, BLOCK, wide), BF16),
            jax.ShapeDtypeStruct((2, BLOCK, wide), BF16),
            half,
            half,
        ],
        *[pltpu.with_memory_space_constraint(array, pltpu.HBM) for array in stored],
        space=pl.BlockSpec(memory_space=pltpu.HBM),
        scratch=[pltpu.VMEM(array.shape, array.dtype) for array in stored]
        + [pltpu.SemaphoreType.DMA((len(stored),))],
        flops=1 << 21,
    )

    pair = (2, extent, BLOCK)
    triple = (3, extent, BLOCK)
    precond, precision, to_down, to_up = call(
        prepare_kernel, [pair, pair, triple, triple],
        right, obs, before, bands, flag, diagonal, local,
    )
    up, down = ring("space", True)
    below = lax.ppermute(to_up, "space", up)
    above = lax.ppermute(to_down, "space", down)
    one, down_two, up_two = call(
        first_kernel, [pair, pair, pair],
        to_down, to_up, below, above, precision, bands, local, into, out,
    )
    below_two = lax.ppermute(up_two, "space", up)
    above_two = lax.ppermute(down_two, "space", down)
    three, four, back, sums = call(
        second_kernel, [pair, pair, (2, 4, HALO, BLOCK), (lax.axis_size("tm"), 1, BLOCK)],
        to_down, to_up, below, above, one, down_two, up_two, below_two, above_two,
        precond, precision, bands, local, into, out,
    )
    back = lax.ppermute(back, "tm", earlier)
    gathered = lax.all_to_all(sums, "tm", 0, 0)
    sums = jnp.sum(gathered, axis=0)
    sent = jnp.broadcast_to(sums[None], (lax.axis_size("space"), 1, BLOCK))
    gathered = lax.all_to_all(sent, "space", 0, 0)
    sums = jnp.sum(gathered, axis=0)
    return tuple(
        call(
            final_kernel, [right_side.shape, right_side.shape],
            flag, sums, to_down, to_up, one, down_two, up_two, three, four, precond, back,
        )
    )


def solution(mesh):
    placed = (
        P("tm", "space"),
        P("tm", "space"),
        P("space", None, None, None),
        P("space", None, None, None),
        P("space", None),
        P(),
        P(),
    )
    return jax.shard_map(
        shards,
        mesh=mesh,
        in_specs=placed,
        out_specs=(P("tm", "space"), P("tm", "space")),
        check_vma=False,
    )
```

```python
import jax
import jax.numpy as jnp
from jax import lax
from jax.experimental import pallas as pl
from jax.experimental.pallas import tpu as pltpu
from jax.sharding import PartitionSpec as P

ITERS = 4
HALO = 2 * ITERS
FRONT = 2 * HALO
BLOCK = 128
CENTRE = 1.0
WIDTH = 0.6
VMEM = pl.BlockSpec(memory_space=pltpu.VMEM)
F32 = jnp.float32
BF16 = jnp.bfloat16
TERMS = ((0, 0, 0), (1, 1, -1), (-1, 1, 0), (2, 2, -2), (-2, 2, 0))


def parts_of(array, count):
    parts = []
    for _ in range(count):
        part = array.astype(BF16)
        parts.append(part)
        array = array - part.astype(F32)
    return parts


def dot(left, right):
    return jnp.dot(left, right, preferred_element_type=F32)


def stacked_product(parts, block):
    rows = parts[0].shape[0]
    product = dot(jnp.concatenate(parts, axis=0), block)
    result = product[:rows]
    for k in range(1, len(parts)):
        result = result + product[k * rows : (k + 1) * rows]
    return result


def local_product(vectors, weights):
    parts = parts_of(jnp.concatenate(vectors, axis=1), 3)
    return stacked_product(parts, weights[0]) + dot(parts[0], weights[1])


def cross_product(vector, block):
    return stacked_product(parts_of(vector, 3), block)


def moved(rows, offset):
    return pltpu.roll(rows, (-offset) % rows.shape[0], 0)


def band_apply(bands, spatial):
    first, second = spatial[:, :BLOCK], spatial[:, BLOCK:]
    result = None
    for index, (offset, _, _) in enumerate(TERMS):
        term = bands[index] * first + bands[5 + index] * second
        if offset:
            term = moved(term, offset)
        result = term if result is None else result + term
    return result


def weights_kernel(
    lists_hbm, pattern_hbm, bands_hbm, right_hbm, obs_hbm, mass_hbm, stiff_hbm,
    bands_ref, flag_ref, diagonal_ref, local_ref, into_ref, out_ref, right_ref, obs_ref,
    lists, pattern, band_rows, right, obs, mass, stiff, arrived,
):
    sources = (lists_hbm, pattern_hbm, bands_hbm, right_hbm, obs_hbm, mass_hbm, stiff_hbm)
    targets = (lists, pattern, band_rows, right, obs, mass, stiff)
    copies = [
        pltpu.make_async_copy(source, target, arrived.at[index])
        for index, (source, target) in enumerate(zip(sources, targets))
    ]
    for copy in copies:
        copy.start()
    for copy in copies[:5]:
        copy.wait()
    time_rows, time_total = right.shape[0], band_rows.shape[2]
    extent = time_rows + FRONT

    first = lax.axis_index("tm") * time_rows - FRONT - 2
    tile = (first + time_total) // BLOCK - time_total // BLOCK
    shift = first - tile * BLOCK
    last_tile = time_total // BLOCK - 1
    lane = lax.broadcasted_iota(jnp.int32, (1, BLOCK), 1)
    time = first + lane
    inside = (time >= 0) & (time < time_total)

    def window(band, matrix):
        halves = []
        for index in (tile, tile + 1):
            index = jnp.clip(index, 0, last_tile)
            start = pl.multiple_of(index * BLOCK, BLOCK)
            row = band_rows[band, :, pl.ds(start, BLOCK)][matrix : matrix + 1]
            halves.append(pltpu.roll(row, (BLOCK - shift) % BLOCK, 1))
        line = jnp.where(lane + shift < BLOCK, halves[0], halves[1])
        return jnp.where(inside, line, 0.0)

    lines = []
    for matrix in range(2):
        rows = [window(band, matrix) for band in range(3)]
        for offset, band, shifted in TERMS:
            line = pltpu.roll(rows[band], (-(2 + shifted)) % BLOCK, 1)
            lines.append(jnp.where(lane >= offset, line, 0.0) if offset > 0 else line)
    valid = jnp.where(inside, 1.0, 0.0)
    lines.append(pltpu.roll(valid, BLOCK - 2, 1))
    count = len(lines)
    lines.append(jnp.zeros((BLOCK - count, BLOCK), F32))
    columns = jnp.concatenate(lines, axis=0).T
    for index in range(count):
        bands_ref[index] = jnp.broadcast_to(
            columns[:extent, index : index + 1], (extent, BLOCK)
        )

    entries = lists[0].astype(F32)
    here = lax.broadcasted_iota(jnp.int32, entries.shape, 1) == lax.axis_index("space")
    low = jnp.sum(jnp.where(here, entries, 0.0), axis=1, keepdims=True)
    low = jnp.where(lax.axis_index("space") % 2 == 0, low, 1.0 - low)
    flag = jnp.broadcast_to(low, (8, BLOCK))
    flag_ref[...] = flag
    swapped = jnp.broadcast_to(low, (BLOCK, BLOCK)) > 0.5
    for ref, source in ((right_ref, right), (obs_ref, obs)):
        one, two = source[:, :BLOCK], source[:, BLOCK:]
        turned = jnp.broadcast_to(low, one.shape) > 0.5
        ref[0] = jnp.where(turned, two, one)
        ref[1] = jnp.where(turned, one, two)
    codes = pattern[...].astype(F32)
    codes = (
        low * codes[1:2] + (1.0 - low) * codes[0:1],
        low * codes[0:1] + (1.0 - low) * codes[1:2],
    )
    own = (low, 1.0 - low)

    for copy in copies[5:]:
        copy.wait()
    eye = lax.broadcasted_iota(jnp.int32, (BLOCK, BLOCK), 0) == lax.broadcasted_iota(
        jnp.int32, (BLOCK, BLOCK), 1
    )
    diagonals = [None] * 4
    for matrix, ref in enumerate((mass, stiff)):

        def block(place, j):
            one, two = ref[place, j].astype(F32), ref[1 - place, j].astype(F32)
            return jnp.where(swapped, two, one)

        stored = [[block(place, j) for j in range(4)] for place in range(2)]
        for place in range(2):
            diagonals[2 * place + matrix] = jnp.sum(
                jnp.where(eye, stored[place][0], 0.0), axis=0, keepdims=True
            )
        for col in range(2):
            lanes = slice((2 * col + matrix) * BLOCK, (2 * col + matrix + 1) * BLOCK)
            for row in range(2):
                total = stored[row][0] if row == col else jnp.zeros((BLOCK, BLOCK), F32)
                for j in (2, 3):
                    named = codes[row][:, j : j + 1] == own[col]
                    total = total + jnp.where(named, 1.0, 0.0) * stored[row][j]
                lead, rest = parts_of(total, 2)
                for k, value in enumerate((lead, rest)):
                    local_ref[k, row * BLOCK : (row + 1) * BLOCK, lanes] = value
        lanes = slice(matrix * BLOCK, (matrix + 1) * BLOCK)
        for place in range(2):
            out_ref[place, :, lanes] = stored[place][1].astype(BF16)
            into_ref[place, :, lanes] = stored[place][1].T.astype(BF16)
    diagonal_ref[...] = jnp.concatenate(diagonals + [jnp.zeros((4, BLOCK), F32)], axis=0)


def stepped(scale, applied, inverse, vector, older):
    result = scale * (inverse * applied - CENTRE * vector)
    return result if older is None else result - older


def prepare_kernel(
    right, obs, before, bands, flag, diagonal, local,
    precond_ref, obs_ref, down_ref, up_ref,
):
    swapped = flag[...] > 0.5

    def extended(middle, start):
        rows = before[start : start + FRONT]
        one, two = rows[:, :BLOCK], rows[:, BLOCK:]
        turned = jnp.concatenate([swapped] * (FRONT // 8), axis=0)
        ends = (jnp.where(turned, two, one), jnp.where(turned, one, two))
        return [jnp.concatenate([ends[k], middle[k]], axis=0) for k in range(2)]

    rhs, precision = extended(right, 0), extended(obs, FRONT)
    valid = bands[10]
    scaled, inverses = [], []
    for place in range(2):
        precond = bands[0] * diagonal[2 * place : 2 * place + 1]
        precond = precond + bands[5] * diagonal[2 * place + 1 : 2 * place + 2]
        precond = precond + precision[place] + (1.0 - valid)
        precond_ref[place] = precond
        obs_ref[place] = precision[place]
        inverses.append(valid / precond)
        scaled.append(rhs[place] * inverses[place])
    spatial = local_product(scaled, local)
    for place, ref in enumerate((down_ref, up_ref)):
        applied = band_apply(bands, spatial[:, 2 * place * BLOCK : 2 * (place + 1) * BLOCK])
        applied = applied + precision[place] * scaled[place]
        ref[0] = scaled[place]
        ref[1] = stepped(1.0 / WIDTH, applied, inverses[place], scaled[place], None)
        ref[2] = inverses[place]


def completed(scale, bands, block, vector, partial, inverse):
    return partial + scale * (inverse * band_apply(bands, cross_product(vector, block)))


def full_step(bands, local, into, vectors, nears, precision, inverses, olders):
    spatial = local_product(vectors, local)
    results = []
    for place in range(2):
        mine = spatial[:, 2 * place * BLOCK : 2 * (place + 1) * BLOCK]
        mine = mine + cross_product(nears[place], into[place])
        applied = band_apply(bands, mine) + precision[place] * vectors[place]
        results.append(
            stepped(2.0 / WIDTH, applied, inverses[place], vectors[place], olders[place])
        )
    return results


def first_kernel(
    down, up, below, above, obs, bands, local, into, out,
    one_ref, down_two_ref, up_two_ref,
):
    own, sides = (down, up), (below, above)
    scale = 1.0 / WIDTH
    inverses = [ref[2] for ref in own]
    vectors = [
        completed(scale, bands, into[k], sides[k][0], own[k][1], inverses[k]) for k in range(2)
    ]
    nears = [
        completed(scale, bands, out[k], own[k][0], sides[k][1], sides[k][2]) for k in range(2)
    ]
    olders = [ref[0] for ref in own]
    two = full_step(bands, local, into, vectors, nears, obs, inverses, olders)
    spatial = local_product(two, local)
    for place, ref in enumerate((down_two_ref, up_two_ref)):
        one_ref[place] = vectors[place]
        applied = band_apply(bands, spatial[:, 2 * place * BLOCK : 2 * (place + 1) * BLOCK])
        applied = applied + obs[place] * two[place]
        ref[0] = two[place]
        ref[1] = stepped(2.0 / WIDTH, applied, inverses[place], two[place], vectors[place])


def second_kernel(
    down, up, below, above, one, down_two, up_two, below_two, above_two, precond, obs,
    bands, local, into, out,
    three_ref, four_ref, back_ref, sums_ref,
):
    own, sides = (down, up), (below, above)
    own_two, sides_two = (down_two, up_two), (below_two, above_two)
    scale = 2.0 / WIDTH
    inverses = [ref[2] for ref in own]
    vectors = [
        completed(scale, bands, into[k], sides_two[k][0], own_two[k][1], inverses[k])
        for k in range(2)
    ]
    nears = [
        completed(scale, bands, out[k], own_two[k][0], sides_two[k][1], sides[k][2])
        for k in range(2)
    ]
    olders = [ref[0] for ref in own_two]
    four = full_step(bands, local, into, vectors, nears, obs, inverses, olders)
    extent = bands.shape[1]
    final = lax.axis_index("tm") == lax.axis_size("tm") - 1
    counted = lax.broadcasted_iota(jnp.int32, (extent - HALO, BLOCK), 0) < extent - FRONT
    counted = jnp.where(counted | final, 1.0, 0.0)
    sums = [0.0] * 14
    for place in range(2):
        three_ref[place] = vectors[place]
        four_ref[place] = four[place]
        basis = (own[place][0], one[place], olders[place], vectors[place], four[place])
        for k in range(4):
            back_ref[place, k] = basis[k + 1][HALO:FRONT]
        basis = [rows[HALO:] for rows in basis]
        weight = counted * precond[place][HALO:]
        index = 0
        for i in range(4):
            weighted = weight * basis[i]
            for j in range(i, 5):
                term = (weighted * basis[j]).reshape(-1, 8, BLOCK)
                sums[index] = sums[index] + jnp.sum(term, axis=0)
                index += 1
    rows = [jnp.sum(part, axis=0, keepdims=True) for part in sums]
    table = jnp.concatenate(rows + [jnp.zeros((2, BLOCK), F32)], axis=0)
    totals = jnp.sum(table, axis=1, keepdims=True)
    slots = lax.broadcasted_iota(jnp.int32, (16, BLOCK), 0) == lax.broadcasted_iota(
        jnp.int32, (16, BLOCK), 1
    )
    line = jnp.sum(jnp.where(slots, totals, 0.0), axis=0, keepdims=True)
    sums_ref[...] = jnp.broadcast_to(line[None], sums_ref.shape)


def added(terms):
    while len(terms) > 1:
        terms = [
            terms[k] + terms[k + 1] if k + 1 < len(terms) else terms[k]
            for k in range(0, len(terms), 2)
        ]
    return terms[0]


def operator(vector, degree):
    result = [[] for _ in range(5)]
    for j in range(degree + 1):
        result[j].append(CENTRE * vector[j])
        if j == 0:
            result[1].append(WIDTH * vector[0])
        else:
            result[j + 1].append((0.5 * WIDTH) * vector[j])
            result[j - 1].append((0.5 * WIDTH) * vector[j])
    return [added(terms) if terms else None for terms in result]


def inner_product(table, left, right):
    terms = []
    for i, a in enumerate(left):
        if a is not None:
            row = [
                table[(min(i, j), max(i, j))] * b for j, b in enumerate(right) if b is not None
            ]
            terms.append(a * added(row))
    return added(terms)


def combined(first, factor, second):
    result = []
    for a, b in zip(first, second):
        if b is None:
            result.append(a)
        else:
            result.append(factor * b if a is None else a + factor * b)
    return result


def final_kernel(
    flag, parts, down, up, one, down_two, up_two, three, four, precond, back,
    solution_ref, residual_ref,
):
    rows = jnp.sum(parts[...], axis=0, keepdims=True)
    lane = lax.broadcasted_iota(jnp.int32, (1, BLOCK), 1)
    table = {}
    index = 0
    for i in range(4):
        for j in range(i, 5):
            table[(i, j)] = jnp.sum(jnp.where(lane == index, rows, 0.0), axis=1, keepdims=True)
            index += 1
    state = [jnp.ones((1, 1), F32)] + [None] * 4
    direction = list(state)
    answer = [None] * 5
    norm_now = table[(0, 0)]
    for iteration in range(ITERS):
        applied = operator(direction, iteration)
        step = norm_now / inner_product(table, direction, applied)
        answer = combined(answer, step, direction)
        state = combined(state, -step, applied)
        if iteration + 1 < ITERS:
            norm_next = inner_product(table, state, state)
            direction = combined(state, norm_next / norm_now, direction)
            norm_now = norm_next
    swapped = flag[0:1] > 0.5
    final = lax.axis_index("tm") == lax.axis_size("tm") - 1
    solutions, residuals = [], []
    for place, (ref, ref_two) in enumerate(((down, down_two), (up, up_two))):
        basis = (ref[0], one[place], ref_two[0], three[place], four[place])
        extent = precond.shape[1]
        start = basis[0][FRONT:]
        basis = [
            jnp.concatenate(
                [
                    rows[FRONT : extent - HALO],
                    jnp.where(final, rows[extent - HALO :], back[place, k]),
                ],
                axis=0,
            )
            for k, rows in enumerate(basis[1:])
        ]
        basis.insert(0, start)
        solutions.append(added([answer[k] * basis[k] for k in range(4)]))
        left = added([state[k] * basis[k] for k in range(5)])
        residuals.append(left * precond[place][FRONT:])
    for ref, pair in ((solution_ref, solutions), (residual_ref, residuals)):
        ref[:, :BLOCK] = jnp.where(swapped, pair[1], pair[0])
        ref[:, BLOCK:] = jnp.where(swapped, pair[0], pair[1])


def call(kernel, shapes, *operands, space=VMEM, scratch=(), flops=0):
    return pl.pallas_call(
        kernel,
        out_shape=[
            shape if isinstance(shape, jax.ShapeDtypeStruct) else jax.ShapeDtypeStruct(shape, F32)
            for shape in shapes
        ],
        in_specs=[space] * len(operands),
        out_specs=[VMEM] * len(shapes),
        scratch_shapes=scratch,
        compiler_params=pltpu.CompilerParams(vmem_limit_bytes=32 * 1024 * 1024),
        cost_estimate=pl.CostEstimate(flops=flops, bytes_accessed=1 << 20, transcendentals=0),
    )(*operands)


def ring(axis, wrap):
    devices = lax.axis_size(axis)
    up = [(i, (i + 1) % devices) for i in range(devices if wrap else devices - 1)]
    return up, [(j, i) for i, j in up]


def shards(
    right_side, obs_precision, mass_blocks, stiff_blocks, block_pattern, send_lists, time_bands
):
    time_rows = right_side.shape[0]
    extent = time_rows + FRONT

    later, earlier = ring("tm", False)
    last = jnp.concatenate([right_side[-FRONT:], obs_precision[-FRONT:]], axis=0)
    before = lax.ppermute(last, "tm", later)

    wide = 2 * BLOCK
    stored = (
        send_lists.transpose(1, 2, 0), block_pattern, time_bands.transpose(1, 0, 2),
        right_side, obs_precision, mass_blocks, stiff_blocks,
    )
    half = (2, time_rows, BLOCK)
    bands, flag, diagonal, local, into, out, right, obs = call(
        weights_kernel,
        [
            (11, extent, BLOCK),
            (8, BLOCK),
            (8, BLOCK),
            jax.ShapeDtypeStruct((2, wide, 2 * wide), BF16),
            jax.ShapeDtypeStruct((2, BLOCK, wide), BF16),
            jax.ShapeDtypeStruct((2, BLOCK, wide), BF16),
            half,
            half,
        ],
        *[pltpu.with_memory_space_constraint(array, pltpu.HBM) for array in stored],
        space=pl.BlockSpec(memory_space=pltpu.HBM),
        scratch=[pltpu.VMEM(array.shape, array.dtype) for array in stored]
        + [pltpu.SemaphoreType.DMA((len(stored),))],
        flops=1 << 21,
    )

    pair = (2, extent, BLOCK)
    triple = (3, extent, BLOCK)
    precond, precision, to_down, to_up = call(
        prepare_kernel, [pair, pair, triple, triple],
        right, obs, before, bands, flag, diagonal, local,
    )
    parts = lax.axis_size("space")
    inner = [(i, i ^ 1) for i in range(parts)]
    outer = [(i, ((i + 1) ^ 1) - 1) for i in range(parts)]
    outer = [(i, j % parts) for i, j in outer]
    first, second = outer, inner
    below = lax.ppermute(to_down, "space", first)
    above = lax.ppermute(to_up, "space", second)
    one, down_two, up_two = call(
        first_kernel, [pair, pair, pair],
        to_down, to_up, below, above, precision, bands, local, into, out,
    )
    below_two = lax.ppermute(down_two, "space", first)
    above_two = lax.ppermute(up_two, "space", second)
    three, four, back, sums = call(
        second_kernel, [pair, pair, (2, 4, HALO, BLOCK), (lax.axis_size("tm"), 1, BLOCK)],
        to_down, to_up, below, above, one, down_two, up_two, below_two, above_two,
        precond, precision, bands, local, into, out,
    )
    back = lax.ppermute(back, "tm", earlier)
    gathered = lax.all_to_all(sums, "tm", 0, 0)
    sums = jnp.sum(gathered, axis=0)
    sent = jnp.broadcast_to(sums[None], (lax.axis_size("space"), 1, BLOCK))
    gathered = lax.all_to_all(sent, "space", 0, 0)
    sums = jnp.sum(gathered, axis=0)
    return tuple(
        call(
            final_kernel, [right_side.shape, right_side.shape],
            flag, sums, to_down, to_up, one, down_two, up_two, three, four, precond, back,
        )
    )


def solution(mesh):
    placed = (
        P("tm", "space"),
        P("tm", "space"),
        P("space", None, None, None),
        P("space", None, None, None),
        P("space", None),
        P(),
        P(),
    )
    return jax.shard_map(
        shards,
        mesh=mesh,
        in_specs=placed,
        out_specs=(P("tm", "space"), P("tm", "space")),
        check_vma=False,
    )
```

```python
import jax
import jax.numpy as jnp
from jax import lax
from jax.experimental import pallas as pl
from jax.experimental.pallas import tpu as pltpu
from jax.sharding import PartitionSpec as P

ITERS = 4
HALO = 2 * ITERS
FRONT = 2 * HALO
BLOCK = 128
CENTRE = 1.0
WIDTH = 0.6
VMEM = pl.BlockSpec(memory_space=pltpu.VMEM)
F32 = jnp.float32
BF16 = jnp.bfloat16
TERMS = ((0, 0, 0), (1, 1, -1), (-1, 1, 0), (2, 2, -2), (-2, 2, 0))


def parts_of(array, count):
    parts = []
    for _ in range(count):
        part = array.astype(BF16)
        parts.append(part)
        array = array - part.astype(F32)
    return parts


def dot(left, right):
    return jnp.dot(left, right, preferred_element_type=F32)


def stacked_product(parts, block):
    rows = parts[0].shape[0]
    product = dot(jnp.concatenate(parts, axis=0), block)
    result = product[:rows]
    for k in range(1, len(parts)):
        result = result + product[k * rows : (k + 1) * rows]
    return result


def local_product(vectors, weights):
    parts = parts_of(jnp.concatenate(vectors, axis=1), 3)
    return stacked_product(parts, weights[0]) + dot(parts[0], weights[1])


def cross_product(vector, block):
    return stacked_product(parts_of(vector, 3), block)


def moved(rows, offset):
    return pltpu.roll(rows, (-offset) % rows.shape[0], 0)


def band_apply(bands, spatial):
    first, second = spatial[:, :BLOCK], spatial[:, BLOCK:]
    result = None
    for index, (offset, _, _) in enumerate(TERMS):
        term = bands[index] * first + bands[5 + index] * second
        if offset:
            term = moved(term, offset)
        result = term if result is None else result + term
    return result


def weights_kernel(
    lists_hbm, pattern_hbm, bands_hbm, right_hbm, obs_hbm, mass_hbm, stiff_hbm,
    bands_ref, flag_ref, diagonal_ref, local_ref, into_ref, out_ref, right_ref, obs_ref,
    lists, pattern, band_rows, right, obs, mass, stiff, arrived,
):
    sources = (lists_hbm, pattern_hbm, bands_hbm, right_hbm, obs_hbm, mass_hbm, stiff_hbm)
    targets = (lists, pattern, band_rows, right, obs, mass, stiff)
    copies = [
        pltpu.make_async_copy(source, target, arrived.at[index])
        for index, (source, target) in enumerate(zip(sources, targets))
    ]
    for copy in copies:
        copy.start()
    for copy in copies[:5]:
        copy.wait()
    time_rows, time_total = right.shape[0], band_rows.shape[2]
    extent = time_rows + FRONT

    first = lax.axis_index("tm") * time_rows - 2
    tile = (first + time_total) // BLOCK - time_total // BLOCK
    shift = first - tile * BLOCK
    last_tile = time_total // BLOCK - 1
    lane = lax.broadcasted_iota(jnp.int32, (1, BLOCK), 1)
    time = first + lane
    inside = (time >= 0) & (time < time_total)

    def window(band, matrix):
        halves = []
        for index in (tile, tile + 1):
            index = jnp.clip(index, 0, last_tile)
            start = pl.multiple_of(index * BLOCK, BLOCK)
            row = band_rows[band, :, pl.ds(start, BLOCK)][matrix : matrix + 1]
            halves.append(pltpu.roll(row, (BLOCK - shift) % BLOCK, 1))
        line = jnp.where(lane + shift < BLOCK, halves[0], halves[1])
        return jnp.where(inside, line, 0.0)

    lines = []
    for matrix in range(2):
        rows = [window(band, matrix) for band in range(3)]
        for offset, band, shifted in TERMS:
            line = pltpu.roll(rows[band], (-(2 + shifted)) % BLOCK, 1)
            lines.append(jnp.where(lane < extent + offset, line, 0.0) if offset < 0 else line)
    valid = jnp.where(inside, 1.0, 0.0)
    lines.append(pltpu.roll(valid, BLOCK - 2, 1))
    count = len(lines)
    lines.append(jnp.zeros((BLOCK - count, BLOCK), F32))
    columns = jnp.concatenate(lines, axis=0).T
    for index in range(count):
        bands_ref[index] = jnp.broadcast_to(
            columns[:extent, index : index + 1], (extent, BLOCK)
        )

    entries = lists[0].astype(F32)
    here = lax.broadcasted_iota(jnp.int32, entries.shape, 1) == lax.axis_index("space")
    low = jnp.sum(jnp.where(here, entries, 0.0), axis=1, keepdims=True)
    turn = lax.axis_index("space") + lax.axis_index("tm")
    low = jnp.where(turn % 2 == 0, low, 1.0 - low)
    flag = jnp.broadcast_to(low, (8, BLOCK))
    flag_ref[...] = flag
    swapped = jnp.broadcast_to(low, (BLOCK, BLOCK)) > 0.5
    for ref, source in ((right_ref, right), (obs_ref, obs)):
        one, two = source[:, :BLOCK], source[:, BLOCK:]
        turned = jnp.broadcast_to(low, one.shape) > 0.5
        ref[0] = jnp.where(turned, two, one)
        ref[1] = jnp.where(turned, one, two)
    codes = pattern[...].astype(F32)
    codes = (
        low * codes[1:2] + (1.0 - low) * codes[0:1],
        low * codes[0:1] + (1.0 - low) * codes[1:2],
    )
    own = (low, 1.0 - low)

    for copy in copies[5:]:
        copy.wait()
    eye = lax.broadcasted_iota(jnp.int32, (BLOCK, BLOCK), 0) == lax.broadcasted_iota(
        jnp.int32, (BLOCK, BLOCK), 1
    )
    diagonals = [None] * 4
    for matrix, ref in enumerate((mass, stiff)):

        def block(place, j):
            one, two = ref[place, j].astype(F32), ref[1 - place, j].astype(F32)
            return jnp.where(swapped, two, one)

        stored = [[block(place, j) for j in range(4)] for place in range(2)]
        for place in range(2):
            diagonals[2 * place + matrix] = jnp.sum(
                jnp.where(eye, stored[place][0], 0.0), axis=0, keepdims=True
            )
        for col in range(2):
            lanes = slice((2 * col + matrix) * BLOCK, (2 * col + matrix + 1) * BLOCK)
            for row in range(2):
                total = stored[row][0] if row == col else jnp.zeros((BLOCK, BLOCK), F32)
                for j in (2, 3):
                    named = codes[row][:, j : j + 1] == own[col]
                    total = total + jnp.where(named, 1.0, 0.0) * stored[row][j]
                lead, rest = parts_of(total, 2)
                for k, value in enumerate((lead, rest)):
                    local_ref[k, row * BLOCK : (row + 1) * BLOCK, lanes] = value
        lanes = slice(matrix * BLOCK, (matrix + 1) * BLOCK)
        for place in range(2):
            out_ref[place, :, lanes] = stored[place][1].astype(BF16)
            into_ref[place, :, lanes] = stored[place][1].T.astype(BF16)
    diagonal_ref[...] = jnp.concatenate(diagonals + [jnp.zeros((4, BLOCK), F32)], axis=0)


def stepped(scale, applied, inverse, vector, older):
    result = scale * (inverse * applied - CENTRE * vector)
    return result if older is None else result - older


def prepare_kernel(
    right, obs, after, bands, flag, diagonal, local,
    precond_ref, obs_ref, down_ref, up_ref,
):
    swapped = flag[...] > 0.5

    def extended(middle, start):
        rows = after[start : start + FRONT]
        one, two = rows[:, :BLOCK], rows[:, BLOCK:]
        turned = jnp.concatenate([swapped] * (FRONT // 8), axis=0)
        ends = (jnp.where(turned, two, one), jnp.where(turned, one, two))
        return [jnp.concatenate([middle[k], ends[k]], axis=0) for k in range(2)]

    rhs, precision = extended(right, 0), extended(obs, FRONT)
    valid = bands[10]
    scaled, inverses = [], []
    for place in range(2):
        precond = bands[0] * diagonal[2 * place : 2 * place + 1]
        precond = precond + bands[5] * diagonal[2 * place + 1 : 2 * place + 2]
        precond = precond + precision[place] + (1.0 - valid)
        precond_ref[place] = precond
        obs_ref[place] = precision[place]
        inverses.append(valid / precond)
        scaled.append(rhs[place] * inverses[place])
    spatial = local_product(scaled, local)
    for place, ref in enumerate((down_ref, up_ref)):
        applied = band_apply(bands, spatial[:, 2 * place * BLOCK : 2 * (place + 1) * BLOCK])
        applied = applied + precision[place] * scaled[place]
        ref[0] = scaled[place]
        ref[1] = stepped(1.0 / WIDTH, applied, inverses[place], scaled[place], None)
        ref[2] = inverses[place]


def completed(scale, bands, block, vector, partial, inverse):
    return partial + scale * (inverse * band_apply(bands, cross_product(vector, block)))


def full_step(bands, local, into, vectors, nears, precision, inverses, olders):
    spatial = local_product(vectors, local)
    results = []
    for place in range(2):
        mine = spatial[:, 2 * place * BLOCK : 2 * (place + 1) * BLOCK]
        mine = mine + cross_product(nears[place], into[place])
        applied = band_apply(bands, mine) + precision[place] * vectors[place]
        results.append(
            stepped(2.0 / WIDTH, applied, inverses[place], vectors[place], olders[place])
        )
    return results


def first_kernel(
    down, up, below, above, obs, bands, local, into, out,
    one_ref, down_two_ref, up_two_ref,
):
    own, sides = (down, up), (below, above)
    scale = 1.0 / WIDTH
    inverses = [ref[2] for ref in own]
    vectors = [
        completed(scale, bands, into[k], sides[k][0], own[k][1], inverses[k]) for k in range(2)
    ]
    nears = [
        completed(scale, bands, out[k], own[k][0], sides[k][1], sides[k][2]) for k in range(2)
    ]
    olders = [ref[0] for ref in own]
    two = full_step(bands, local, into, vectors, nears, obs, inverses, olders)
    spatial = local_product(two, local)
    for place, ref in enumerate((down_two_ref, up_two_ref)):
        one_ref[place] = vectors[place]
        applied = band_apply(bands, spatial[:, 2 * place * BLOCK : 2 * (place + 1) * BLOCK])
        applied = applied + obs[place] * two[place]
        ref[0] = two[place]
        ref[1] = stepped(2.0 / WIDTH, applied, inverses[place], two[place], vectors[place])


def second_kernel(
    down, up, below, above, one, down_two, up_two, below_two, above_two, precond, obs,
    bands, local, into, out,
    three_ref, four_ref, back_ref, sums_ref,
):
    own, sides = (down, up), (below, above)
    own_two, sides_two = (down_two, up_two), (below_two, above_two)
    scale = 2.0 / WIDTH
    inverses = [ref[2] for ref in own]
    vectors = [
        completed(scale, bands, into[k], sides_two[k][0], own_two[k][1], inverses[k])
        for k in range(2)
    ]
    nears = [
        completed(scale, bands, out[k], own_two[k][0], sides_two[k][1], sides[k][2])
        for k in range(2)
    ]
    olders = [ref[0] for ref in own_two]
    four = full_step(bands, local, into, vectors, nears, obs, inverses, olders)
    extent = bands.shape[1]
    initial = lax.axis_index("tm") == 0
    counted = lax.broadcasted_iota(jnp.int32, (extent - HALO, BLOCK), 0) >= HALO
    counted = jnp.where(counted | initial, 1.0, 0.0)
    sums = [0.0] * 14
    for place in range(2):
        three_ref[place] = vectors[place]
        four_ref[place] = four[place]
        basis = (own[place][0], one[place], olders[place], vectors[place], four[place])
        for k in range(4):
            back_ref[place, k] = basis[k + 1][extent - FRONT : extent - HALO]
        basis = [rows[: extent - HALO] for rows in basis]
        weight = counted * precond[place][: extent - HALO]
        index = 0
        for i in range(4):
            weighted = weight * basis[i]
            for j in range(i, 5):
                term = (weighted * basis[j]).reshape(-1, 8, BLOCK)
                sums[index] = sums[index] + jnp.sum(term, axis=0)
                index += 1
    rows = [jnp.sum(part, axis=0, keepdims=True) for part in sums]
    table = jnp.concatenate(rows + [jnp.zeros((2, BLOCK), F32)], axis=0)
    totals = jnp.sum(table, axis=1, keepdims=True)
    slots = lax.broadcasted_iota(jnp.int32, (16, BLOCK), 0) == lax.broadcasted_iota(
        jnp.int32, (16, BLOCK), 1
    )
    line = jnp.sum(jnp.where(slots, totals, 0.0), axis=0, keepdims=True)
    sums_ref[...] = jnp.broadcast_to(line[None], sums_ref.shape)


def added(terms):
    while len(terms) > 1:
        terms = [
            terms[k] + terms[k + 1] if k + 1 < len(terms) else terms[k]
            for k in range(0, len(terms), 2)
        ]
    return terms[0]


def operator(vector, degree):
    result = [[] for _ in range(5)]
    for j in range(degree + 1):
        result[j].append(CENTRE * vector[j])
        if j == 0:
            result[1].append(WIDTH * vector[0])
        else:
            result[j + 1].append((0.5 * WIDTH) * vector[j])
            result[j - 1].append((0.5 * WIDTH) * vector[j])
    return [added(terms) if terms else None for terms in result]


def inner_product(table, left, right):
    terms = []
    for i, a in enumerate(left):
        if a is not None:
            row = [
                table[(min(i, j), max(i, j))] * b for j, b in enumerate(right) if b is not None
            ]
            terms.append(a * added(row))
    return added(terms)


def combined(first, factor, second):
    result = []
    for a, b in zip(first, second):
        if b is None:
            result.append(a)
        else:
            result.append(factor * b if a is None else a + factor * b)
    return result


def final_kernel(
    flag, parts, down, up, one, down_two, up_two, three, four, precond, back,
    solution_ref, residual_ref,
):
    rows = jnp.sum(parts[...], axis=0, keepdims=True)
    lane = lax.broadcasted_iota(jnp.int32, (1, BLOCK), 1)
    table = {}
    index = 0
    for i in range(4):
        for j in range(i, 5):
            table[(i, j)] = jnp.sum(jnp.where(lane == index, rows, 0.0), axis=1, keepdims=True)
            index += 1
    state = [jnp.ones((1, 1), F32)] + [None] * 4
    direction = list(state)
    answer = [None] * 5
    norm_now = table[(0, 0)]
    for iteration in range(ITERS):
        applied = operator(direction, iteration)
        step = norm_now / inner_product(table, direction, applied)
        answer = combined(answer, step, direction)
        state = combined(state, -step, applied)
        if iteration + 1 < ITERS:
            norm_next = inner_product(table, state, state)
            direction = combined(state, norm_next / norm_now, direction)
            norm_now = norm_next
    swapped = flag[0:1] > 0.5
    initial = lax.axis_index("tm") == 0
    solutions, residuals = [], []
    for place, (ref, ref_two) in enumerate(((down, down_two), (up, up_two))):
        basis = (ref[0], one[place], ref_two[0], three[place], four[place])
        extent = precond.shape[1]
        start = basis[0][: extent - FRONT]
        basis = [
            jnp.concatenate(
                [
                    jnp.where(initial, rows[:HALO], back[1 - place, k]),
                    rows[HALO : extent - FRONT],
                ],
                axis=0,
            )
            for k, rows in enumerate(basis[1:])
        ]
        basis.insert(0, start)
        solutions.append(added([answer[k] * basis[k] for k in range(4)]))
        left = added([state[k] * basis[k] for k in range(5)])
        residuals.append(left * precond[place][: extent - FRONT])
    for ref, pair in ((solution_ref, solutions), (residual_ref, residuals)):
        ref[:, :BLOCK] = jnp.where(swapped, pair[1], pair[0])
        ref[:, BLOCK:] = jnp.where(swapped, pair[0], pair[1])


def call(kernel, shapes, *operands, space=VMEM, scratch=(), flops=0):
    return pl.pallas_call(
        kernel,
        out_shape=[
            shape if isinstance(shape, jax.ShapeDtypeStruct) else jax.ShapeDtypeStruct(shape, F32)
            for shape in shapes
        ],
        in_specs=[space] * len(operands),
        out_specs=[VMEM] * len(shapes),
        scratch_shapes=scratch,
        compiler_params=pltpu.CompilerParams(vmem_limit_bytes=32 * 1024 * 1024),
        cost_estimate=pl.CostEstimate(flops=flops, bytes_accessed=1 << 20, transcendentals=0),
    )(*operands)


def ring(axis, wrap):
    devices = lax.axis_size(axis)
    up = [(i, (i + 1) % devices) for i in range(devices if wrap else devices - 1)]
    return up, [(j, i) for i, j in up]


def shards(
    right_side, obs_precision, mass_blocks, stiff_blocks, block_pattern, send_lists, time_bands
):
    time_rows = right_side.shape[0]
    extent = time_rows + FRONT

    later, earlier = ring("tm", False)
    first = jnp.concatenate([right_side[:FRONT], obs_precision[:FRONT]], axis=0)
    after = lax.ppermute(first, "tm", earlier)

    wide = 2 * BLOCK
    stored = (
        send_lists.transpose(1, 2, 0), block_pattern, time_bands.transpose(1, 0, 2),
        right_side, obs_precision, mass_blocks, stiff_blocks,
    )
    half = (2, time_rows, BLOCK)
    bands, flag, diagonal, local, into, out, right, obs = call(
        weights_kernel,
        [
            (11, extent, BLOCK),
            (8, BLOCK),
            (8, BLOCK),
            jax.ShapeDtypeStruct((2, wide, 2 * wide), BF16),
            jax.ShapeDtypeStruct((2, BLOCK, wide), BF16),
            jax.ShapeDtypeStruct((2, BLOCK, wide), BF16),
            half,
            half,
        ],
        *[pltpu.with_memory_space_constraint(array, pltpu.HBM) for array in stored],
        space=pl.BlockSpec(memory_space=pltpu.HBM),
        scratch=[pltpu.VMEM(array.shape, array.dtype) for array in stored]
        + [pltpu.SemaphoreType.DMA((len(stored),))],
        flops=1 << 21,
    )

    pair = (2, extent, BLOCK)
    triple = (3, extent, BLOCK)
    precond, precision, to_down, to_up = call(
        prepare_kernel, [pair, pair, triple, triple],
        right, obs, after, bands, flag, diagonal, local,
    )
    parts = lax.axis_size("space")
    swaps = ([], [])
    for slab in range(lax.axis_size("tm")):
        for i in range(parts):
            outer = (((i + 1) ^ 1) - 1) % parts
            order = (outer, i ^ 1) if slab % 2 == 0 else (i ^ 1, outer)
            for pairs, j in zip(swaps, order):
                pairs.append((slab * parts + i, slab * parts + j))
    first, second = swaps
    both = ("tm", "space")
    below = lax.ppermute(to_down, both, first)
    above = lax.ppermute(to_up, both, second)
    one, down_two, up_two = call(
        first_kernel, [pair, pair, pair],
        to_down, to_up, below, above, precision, bands, local, into, out,
    )
    below_two = lax.ppermute(down_two, both, first)
    above_two = lax.ppermute(up_two, both, second)
    three, four, back, sums = call(
        second_kernel, [pair, pair, (2, 4, HALO, BLOCK), (lax.axis_size("tm"), 1, BLOCK)],
        to_down, to_up, below, above, one, down_two, up_two, below_two, above_two,
        precond, precision, bands, local, into, out,
    )
    back = lax.ppermute(back, "tm", later)
    gathered = lax.all_to_all(sums, "tm", 0, 0)
    sums = jnp.sum(gathered, axis=0)
    sent = jnp.broadcast_to(sums[None], (lax.axis_size("space"), 1, BLOCK))
    gathered = lax.all_to_all(sent, "space", 0, 0)
    sums = jnp.sum(gathered, axis=0)
    return tuple(
        call(
            final_kernel, [right_side.shape, right_side.shape],
            flag, sums, to_down, to_up, one, down_two, up_two, three, four, precond, back,
        )
    )


def solution(mesh):
    placed = (
        P("tm", "space"),
        P("tm", "space"),
        P("space", None, None, None),
        P("space", None, None, None),
        P("space", None),
        P(),
        P(),
    )
    return jax.shard_map(
        shards,
        mesh=mesh,
        in_specs=placed,
        out_specs=(P("tm", "space"), P("tm", "space")),
        check_vma=False,
    )
```

```python
import jax
import jax.numpy as jnp
from jax import lax
from jax.experimental import pallas as pl
from jax.experimental.pallas import tpu as pltpu
from jax.sharding import PartitionSpec as P

ITERS = 4
HALO = 2 * ITERS
FRONT = 2 * HALO
BLOCK = 128
CENTRE = 1.0
WIDTH = 0.6
VMEM = pl.BlockSpec(memory_space=pltpu.VMEM)
F32 = jnp.float32
BF16 = jnp.bfloat16
TERMS = ((0, 0, 0), (1, 1, -1), (-1, 1, 0), (2, 2, -2), (-2, 2, 0))


def parts_of(array, count):
    parts = []
    for _ in range(count):
        part = array.astype(BF16)
        parts.append(part)
        array = array - part.astype(F32)
    return parts


def dot(left, right):
    return jnp.dot(left, right, preferred_element_type=F32)


def stacked_product(parts, block):
    rows = parts[0].shape[0]
    product = dot(jnp.concatenate(parts, axis=0), block)
    result = product[:rows]
    for k in range(1, len(parts)):
        result = result + product[k * rows : (k + 1) * rows]
    return result


def local_product(vectors, weights):
    parts = parts_of(jnp.concatenate(vectors, axis=1), 3)
    return stacked_product(parts, weights[0]) + dot(parts[0], weights[1])


def cross_product(vector, block):
    return stacked_product(parts_of(vector, 3), block)


def moved(rows, offset):
    return pltpu.roll(rows, (-offset) % rows.shape[0], 0)


def band_apply(bands, spatial):
    first, second = spatial[:, :BLOCK], spatial[:, BLOCK:]
    result = None
    for index, (offset, _, _) in enumerate(TERMS):
        term = bands[index] * first + bands[5 + index] * second
        if offset:
            term = moved(term, offset)
        result = term if result is None else result + term
    return result


def weights_kernel(
    lists_hbm, pattern_hbm, bands_hbm, right_hbm, obs_hbm, mass_hbm, stiff_hbm,
    bands_ref, flag_ref, diagonal_ref, local_ref, into_ref, out_ref, right_ref, obs_ref,
    lists, pattern, band_rows, right, obs, mass, stiff, arrived,
):
    sources = (lists_hbm, pattern_hbm, bands_hbm, right_hbm, obs_hbm, mass_hbm, stiff_hbm)
    targets = (lists, pattern, band_rows, right, obs, mass, stiff)
    copies = [
        pltpu.make_async_copy(source, target, arrived.at[index])
        for index, (source, target) in enumerate(zip(sources, targets))
    ]
    for copy in copies:
        copy.start()
    for copy in copies[:5]:
        copy.wait()
    time_rows, time_total = right.shape[0], band_rows.shape[2]
    extent = time_rows + FRONT

    first = lax.axis_index("tm") * time_rows - 2
    tile = (first + time_total) // BLOCK - time_total // BLOCK
    shift = first - tile * BLOCK
    last_tile = time_total // BLOCK - 1
    lane = lax.broadcasted_iota(jnp.int32, (1, BLOCK), 1)
    time = first + lane
    inside = (time >= 0) & (time < time_total)

    def window(band, matrix):
        halves = []
        for index in (tile, tile + 1):
            index = jnp.clip(index, 0, last_tile)
            start = pl.multiple_of(index * BLOCK, BLOCK)
            row = band_rows[band, :, pl.ds(start, BLOCK)][matrix : matrix + 1]
            halves.append(pltpu.roll(row, (BLOCK - shift) % BLOCK, 1))
        line = jnp.where(lane + shift < BLOCK, halves[0], halves[1])
        return jnp.where(inside, line, 0.0)

    lines = []
    for matrix in range(2):
        rows = [window(band, matrix) for band in range(3)]
        for offset, band, shifted in TERMS:
            line = pltpu.roll(rows[band], (-(2 + shifted)) % BLOCK, 1)
            lines.append(jnp.where(lane < extent + offset, line, 0.0) if offset < 0 else line)
    valid = jnp.where(inside, 1.0, 0.0)
    lines.append(pltpu.roll(valid, BLOCK - 2, 1))
    count = len(lines)
    lines.append(jnp.zeros((BLOCK - count, BLOCK), F32))
    columns = jnp.concatenate(lines, axis=0).T
    for index in range(count):
        bands_ref[index] = jnp.broadcast_to(
            columns[:extent, index : index + 1], (extent, BLOCK)
        )

    entries = lists[0].astype(F32)
    here = lax.broadcasted_iota(jnp.int32, entries.shape, 1) == lax.axis_index("space")
    low = jnp.sum(jnp.where(here, entries, 0.0), axis=1, keepdims=True)
    turn = lax.axis_index("space") + lax.axis_index("tm")
    low = jnp.where(turn % 2 == 0, low, 1.0 - low)
    flag = jnp.broadcast_to(low, (8, BLOCK))
    flag_ref[...] = flag
    swapped = jnp.broadcast_to(low, (BLOCK, BLOCK)) > 0.5
    for ref, source in ((right_ref, right), (obs_ref, obs)):
        one, two = source[:, :BLOCK], source[:, BLOCK:]
        turned = jnp.broadcast_to(low, one.shape) > 0.5
        ref[0] = jnp.where(turned, two, one)
        ref[1] = jnp.where(turned, one, two)
    codes = pattern[...].astype(F32)
    codes = (
        low * codes[1:2] + (1.0 - low) * codes[0:1],
        low * codes[0:1] + (1.0 - low) * codes[1:2],
    )
    own = (low, 1.0 - low)

    for copy in copies[5:]:
        copy.wait()
    eye = lax.broadcasted_iota(jnp.int32, (BLOCK, BLOCK), 0) == lax.broadcasted_iota(
        jnp.int32, (BLOCK, BLOCK), 1
    )
    diagonals = [None] * 4
    for matrix, ref in enumerate((mass, stiff)):

        def block(place, j):
            one, two = ref[place, j].astype(F32), ref[1 - place, j].astype(F32)
            return jnp.where(swapped, two, one)

        stored = [[block(place, j) for j in range(4)] for place in range(2)]
        for place in range(2):
            diagonals[2 * place + matrix] = jnp.sum(
                jnp.where(eye, stored[place][0], 0.0), axis=0, keepdims=True
            )
        for col in range(2):
            lanes = slice((2 * col + matrix) * BLOCK, (2 * col + matrix + 1) * BLOCK)
            for row in range(2):
                total = stored[row][0] if row == col else jnp.zeros((BLOCK, BLOCK), F32)
                for j in (2, 3):
                    named = codes[row][:, j : j + 1] == own[col]
                    total = total + jnp.where(named, 1.0, 0.0) * stored[row][j]
                lead, rest = parts_of(total, 2)
                for k, value in enumerate((lead, rest)):
                    local_ref[k, row * BLOCK : (row + 1) * BLOCK, lanes] = value
        lanes = slice(matrix * BLOCK, (matrix + 1) * BLOCK)
        for place in range(2):
            out_ref[place, :, lanes] = stored[place][1].astype(BF16)
            into_ref[place, :, lanes] = stored[place][1].T.astype(BF16)
    diagonal_ref[...] = jnp.concatenate(diagonals + [jnp.zeros((4, BLOCK), F32)], axis=0)


def stepped(scale, applied, inverse, vector, older):
    result = scale * (inverse * applied - CENTRE * vector)
    return result if older is None else result - older


def prepare_kernel(
    right, obs, after, bands, flag, diagonal, local,
    precond_ref, obs_ref, down_ref, up_ref,
):
    swapped = flag[...] > 0.5

    def extended(middle, start):
        rows = after[start : start + FRONT]
        one, two = rows[:, :BLOCK], rows[:, BLOCK:]
        turned = jnp.concatenate([swapped] * (FRONT // 8), axis=0)
        ends = (jnp.where(turned, two, one), jnp.where(turned, one, two))
        return [jnp.concatenate([middle[k], ends[k]], axis=0) for k in range(2)]

    rhs, precision = extended(right, 0), extended(obs, FRONT)
    valid = bands[10]
    scaled, inverses = [], []
    for place in range(2):
        precond = bands[0] * diagonal[2 * place : 2 * place + 1]
        precond = precond + bands[5] * diagonal[2 * place + 1 : 2 * place + 2]
        precond = precond + precision[place] + (1.0 - valid)
        precond_ref[place] = precond
        obs_ref[place] = precision[place]
        inverses.append(valid / precond)
        scaled.append(rhs[place] * inverses[place])
    spatial = local_product(scaled, local)
    for place, ref in enumerate((down_ref, up_ref)):
        applied = band_apply(bands, spatial[:, 2 * place * BLOCK : 2 * (place + 1) * BLOCK])
        applied = applied + precision[place] * scaled[place]
        ref[0] = scaled[place]
        ref[1] = stepped(1.0 / WIDTH, applied, inverses[place], scaled[place], None)
        ref[2] = inverses[place]


def completed(scale, bands, block, vector, partial, inverse):
    return partial + scale * (inverse * band_apply(bands, cross_product(vector, block)))


def full_step(bands, local, into, vectors, nears, precision, inverses, olders):
    spatial = local_product(vectors, local)
    results = []
    for place in range(2):
        mine = spatial[:, 2 * place * BLOCK : 2 * (place + 1) * BLOCK]
        mine = mine + cross_product(nears[place], into[place])
        applied = band_apply(bands, mine) + precision[place] * vectors[place]
        results.append(
            stepped(2.0 / WIDTH, applied, inverses[place], vectors[place], olders[place])
        )
    return results


def first_kernel(
    down, up, below, above, obs, bands, local, into, out,
    one_ref, down_two_ref, up_two_ref,
):
    own, sides = (down, up), (below, above)
    scale = 1.0 / WIDTH
    inverses = [ref[2] for ref in own]
    vectors = [
        completed(scale, bands, into[k], sides[k][0], own[k][1], inverses[k]) for k in range(2)
    ]
    nears = [
        completed(scale, bands, out[k], own[k][0], sides[k][1], sides[k][2]) for k in range(2)
    ]
    olders = [ref[0] for ref in own]
    two = full_step(bands, local, into, vectors, nears, obs, inverses, olders)
    spatial = local_product(two, local)
    for place, ref in enumerate((down_two_ref, up_two_ref)):
        one_ref[place] = vectors[place]
        applied = band_apply(bands, spatial[:, 2 * place * BLOCK : 2 * (place + 1) * BLOCK])
        applied = applied + obs[place] * two[place]
        ref[0] = two[place]
        ref[1] = stepped(2.0 / WIDTH, applied, inverses[place], two[place], vectors[place])


def second_kernel(
    down, up, below, above, one, down_two, up_two, below_two, above_two, precond, obs,
    bands, local, into, out,
    three_ref, four_ref, back_ref, sums_ref,
):
    own, sides = (down, up), (below, above)
    own_two, sides_two = (down_two, up_two), (below_two, above_two)
    scale = 2.0 / WIDTH
    inverses = [ref[2] for ref in own]
    vectors = [
        completed(scale, bands, into[k], sides_two[k][0], own_two[k][1], inverses[k])
        for k in range(2)
    ]
    nears = [
        completed(scale, bands, out[k], own_two[k][0], sides_two[k][1], sides[k][2])
        for k in range(2)
    ]
    olders = [ref[0] for ref in own_two]
    four = full_step(bands, local, into, vectors, nears, obs, inverses, olders)
    extent = bands.shape[1]
    initial = lax.axis_index("tm") == 0
    counted = lax.broadcasted_iota(jnp.int32, (extent - HALO, BLOCK), 0) >= HALO
    counted = jnp.where(counted | initial, 1.0, 0.0)
    sums = [0.0] * 14
    for place in range(2):
        three_ref[place] = vectors[place]
        four_ref[place] = four[place]
        basis = (own[place][0], one[place], olders[place], vectors[place], four[place])
        for k in range(4):
            back_ref[place, k] = basis[k + 1][extent - FRONT : extent - HALO]
        basis = [rows[: extent - HALO] for rows in basis]
        weight = counted * precond[place][: extent - HALO]
        index = 0
        for i in range(4):
            weighted = weight * basis[i]
            for j in range(i, 5):
                term = (weighted * basis[j]).reshape(-1, 8, BLOCK)
                sums[index] = sums[index] + jnp.sum(term, axis=0)
                index += 1
    rows = [jnp.sum(part, axis=0, keepdims=True) for part in sums]
    table = jnp.concatenate(rows + [jnp.zeros((2, BLOCK), F32)], axis=0)
    totals = jnp.sum(table, axis=1, keepdims=True)
    slots = lax.broadcasted_iota(jnp.int32, (16, BLOCK), 0) == lax.broadcasted_iota(
        jnp.int32, (16, BLOCK), 1
    )
    line = jnp.sum(jnp.where(slots, totals, 0.0), axis=0, keepdims=True)
    sums_ref[...] = jnp.broadcast_to(line[None], sums_ref.shape)


def added(terms):
    while len(terms) > 1:
        terms = [
            terms[k] + terms[k + 1] if k + 1 < len(terms) else terms[k]
            for k in range(0, len(terms), 2)
        ]
    return terms[0]


def operator(vector, degree):
    result = [[] for _ in range(5)]
    for j in range(degree + 1):
        result[j].append(CENTRE * vector[j])
        if j == 0:
            result[1].append(WIDTH * vector[0])
        else:
            result[j + 1].append((0.5 * WIDTH) * vector[j])
            result[j - 1].append((0.5 * WIDTH) * vector[j])
    return [added(terms) if terms else None for terms in result]


def inner_product(table, left, right):
    terms = []
    for i, a in enumerate(left):
        if a is not None:
            row = [
                table[(min(i, j), max(i, j))] * b for j, b in enumerate(right) if b is not None
            ]
            terms.append(a * added(row))
    return added(terms)


def combined(first, factor, second):
    result = []
    for a, b in zip(first, second):
        if b is None:
            result.append(a)
        else:
            result.append(factor * b if a is None else a + factor * b)
    return result


def final_kernel(
    flag, parts, down, up, one, down_two, up_two, three, four, precond, back,
    solution_ref, residual_ref,
):
    rows = jnp.sum(parts[...], axis=0, keepdims=True)
    lane = lax.broadcasted_iota(jnp.int32, (1, BLOCK), 1)
    table = {}
    index = 0
    for i in range(4):
        for j in range(i, 5):
            table[(i, j)] = jnp.sum(jnp.where(lane == index, rows, 0.0), axis=1, keepdims=True)
            index += 1
    state = [jnp.ones((1, 1), F32)] + [None] * 4
    direction = list(state)
    answer = [None] * 5
    norm_now = table[(0, 0)]
    for iteration in range(ITERS):
        applied = operator(direction, iteration)
        step = norm_now / inner_product(table, direction, applied)
        answer = combined(answer, step, direction)
        state = combined(state, -step, applied)
        if iteration + 1 < ITERS:
            norm_next = inner_product(table, state, state)
            direction = combined(state, norm_next / norm_now, direction)
            norm_now = norm_next
    swapped = flag[0:1] > 0.5
    initial = lax.axis_index("tm") == 0
    solutions, residuals = [], []
    for place, (ref, ref_two) in enumerate(((down, down_two), (up, up_two))):
        basis = (ref[0], one[place], ref_two[0], three[place], four[place])
        extent = precond.shape[1]
        start = basis[0][: extent - FRONT]
        basis = [
            jnp.concatenate(
                [
                    jnp.where(initial, rows[:HALO], back[1 - place, k]),
                    rows[HALO : extent - FRONT],
                ],
                axis=0,
            )
            for k, rows in enumerate(basis[1:])
        ]
        basis.insert(0, start)
        solutions.append(added([answer[k] * basis[k] for k in range(4)]))
        left = added([state[k] * basis[k] for k in range(5)])
        residuals.append(left * precond[place][: extent - FRONT])
    for ref, pair in ((solution_ref, solutions), (residual_ref, residuals)):
        ref[:, :BLOCK] = jnp.where(swapped, pair[1], pair[0])
        ref[:, BLOCK:] = jnp.where(swapped, pair[0], pair[1])


def call(kernel, shapes, *operands, space=VMEM, scratch=(), flops=0):
    return pl.pallas_call(
        kernel,
        out_shape=[
            shape if isinstance(shape, jax.ShapeDtypeStruct) else jax.ShapeDtypeStruct(shape, F32)
            for shape in shapes
        ],
        in_specs=[space] * len(operands),
        out_specs=[VMEM] * len(shapes),
        scratch_shapes=scratch,
        compiler_params=pltpu.CompilerParams(vmem_limit_bytes=32 * 1024 * 1024),
        cost_estimate=pl.CostEstimate(flops=flops, bytes_accessed=1 << 20, transcendentals=0),
    )(*operands)


def ring(axis, wrap):
    devices = lax.axis_size(axis)
    up = [(i, (i + 1) % devices) for i in range(devices if wrap else devices - 1)]
    return up, [(j, i) for i, j in up]


def shards(
    right_side, obs_precision, mass_blocks, stiff_blocks, block_pattern, send_lists, time_bands
):
    time_rows = right_side.shape[0]
    extent = time_rows + FRONT

    later, earlier = ring("tm", False)
    first = jnp.concatenate([right_side[:FRONT], obs_precision[:FRONT]], axis=0)
    after = lax.ppermute(first, "tm", earlier)

    wide = 2 * BLOCK
    stored = (
        send_lists.transpose(1, 2, 0), block_pattern, time_bands.transpose(1, 0, 2),
        right_side, obs_precision, mass_blocks, stiff_blocks,
    )
    half = (2, time_rows, BLOCK)
    bands, flag, diagonal, local, into, out, right, obs = call(
        weights_kernel,
        [
            (11, extent, BLOCK),
            (8, BLOCK),
            (8, BLOCK),
            jax.ShapeDtypeStruct((2, wide, 2 * wide), BF16),
            jax.ShapeDtypeStruct((2, BLOCK, wide), BF16),
            jax.ShapeDtypeStruct((2, BLOCK, wide), BF16),
            half,
            half,
        ],
        *[pltpu.with_memory_space_constraint(array, pltpu.HBM) for array in stored],
        space=pl.BlockSpec(memory_space=pltpu.HBM),
        scratch=[pltpu.VMEM(array.shape, array.dtype) for array in stored]
        + [pltpu.SemaphoreType.DMA((len(stored),))],
        flops=1 << 21,
    )

    pair = (2, extent, BLOCK)
    triple = (3, extent, BLOCK)
    precond, precision, to_down, to_up = call(
        prepare_kernel, [pair, pair, triple, triple],
        right, obs, after, bands, flag, diagonal, local,
    )
    parts = lax.axis_size("space")
    swaps = ([], [])
    for slab in range(lax.axis_size("tm")):
        for i in range(parts):
            outer = (((i + 1) ^ 1) - 1) % parts
            order = (outer, i ^ 1) if slab % 2 == 0 else (i ^ 1, outer)
            for pairs, j in zip(swaps, order):
                pairs.append((slab * parts + i, slab * parts + j))
    first, second = swaps
    both = ("tm", "space")
    below = lax.ppermute(to_down, both, first)
    above = lax.ppermute(to_up, both, second)
    one, down_two, up_two = call(
        first_kernel, [pair, pair, pair],
        to_down, to_up, below, above, precision, bands, local, into, out,
    )
    even = lax.axis_index("tm") % 2 == 0
    outer = [(i, (((i + 1) ^ 1) - 1) % parts) for i in range(parts)]
    inner = [(i, i ^ 1) for i in range(parts)]
    came_outer = lax.ppermute(jnp.where(even, down_two, up_two), "space", outer)
    came_inner = lax.ppermute(jnp.where(even, up_two, down_two), "space", inner)
    below_two = jnp.where(even, came_outer, came_inner)
    above_two = jnp.where(even, came_inner, came_outer)
    three, four, back, sums = call(
        second_kernel, [pair, pair, (2, 4, HALO, BLOCK), (lax.axis_size("tm"), 1, BLOCK)],
        to_down, to_up, below, above, one, down_two, up_two, below_two, above_two,
        precond, precision, bands, local, into, out,
    )
    back = lax.ppermute(back, "tm", later)
    gathered = lax.all_to_all(sums, "tm", 0, 0)
    sums = jnp.sum(gathered, axis=0)
    sent = jnp.broadcast_to(sums[None], (lax.axis_size("space"), 1, BLOCK))
    gathered = lax.all_to_all(sent, "space", 0, 0)
    sums = jnp.sum(gathered, axis=0)
    return tuple(
        call(
            final_kernel, [right_side.shape, right_side.shape],
            flag, sums, to_down, to_up, one, down_two, up_two, three, four, precond, back,
        )
    )


def solution(mesh):
    placed = (
        P("tm", "space"),
        P("tm", "space"),
        P("space", None, None, None),
        P("space", None, None, None),
        P("space", None),
        P(),
        P(),
    )
    return jax.shard_map(
        shards,
        mesh=mesh,
        in_specs=placed,
        out_specs=(P("tm", "space"), P("tm", "space")),
        check_vma=False,
    )
```
